512 devices in a mesh: ent: 64 (over z, y), rel: 8 (over x, core).
Axes of the slice: x: 4, y: 8, z: 8, core: 2. Of those that a mesh axis runs over, the one named last changes fastest.
Arguments:
- features: bfloat16 [16384, 256], P('ent'), may hold values from -6 to 6
- basis_stack: bfloat16 [64, 256, 256], P('rel'), may hold values from -0.375 to 0.375
- coeffs: float32 [1300, 64], P(None, 'rel'), may hold values from -0.75 to 0.75
- self_weight: bfloat16 [256, 256], P(None, 'rel'), may hold values from -0.375 to 0.375
- src_row: int32 [4096, 32], P('ent'), may hold values from 0 to 255
- dst_row: int32 [4096, 32], P('ent'), may hold values from 0 to 255
- rel_id: int32 [4096, 32], P('ent'), may hold values from 0 to 1299
- edge_weight: float32 [4096, 32], P('ent'), may hold values from 0.05 to 1
- counts: int32 [64, 64], P('ent'), may hold values from 1 to 32, as said below
- out_grad: bfloat16 [16384, 256], P('ent', 'rel'), may hold values from -6 to 6
Outputs:
- layer_out: bfloat16 [16384, 256], P('ent', 'rel')
- input_grad: float32 [16384, 256], P('ent', 'rel')
- coef_grad: float32 [1300, 64], P(None, 'rel')
- basis_grad: float32 [64, 256, 256], P('rel')
- self_grad: float32 [256, 256], P(None, 'rel')
The draws below stay inside these ranges and needn't reach their ends.
Inputs may be any that keep to these rules, and one draw needn't show every extreme that they name: Slots at or beyond counts[s, d] are padding. Some destination shard receives 32 live slots from every source shard.
All inputs are finite; a program needn't handle non-finite values.
Results may differ from the reference program's by a relative error of at most 0.013.
Values may be sent and summed in bfloat16 or wider, within the bound.
No kernel may reach another device: no remote copies, remote signals or barrier semaphores. Data moves between devices by JAX's collectives and lax.ppermute only.
A program may use at most 64 MiB of HBM per device.

```python
import math
import jax
import jax.numpy as jnp
import numpy as np
from jax import lax

D = 256
NB = 64
R = 1300
ENT_DEV = 256
CAP = 32
SHARDS = 64
N = 16384
PAIRS = 4096
GROUP_BASES = 8
N_REL = 8


def draw_counts(key, part):
    key = jax.random.fold_in(key, 11)
    key_low, key_heavy, key_pick = jax.random.split(key, 3)
    light = jax.random.randint(key_low, (SHARDS, SHARDS), 1, CAP // 2 + 1)
    heavy_dest = jax.random.randint(key_heavy, (SHARDS,), 0, 8) == 0
    forced = jax.random.randint(key_pick, (), 0, SHARDS)
    heavy_dest = heavy_dest | (jnp.arange(SHARDS, dtype=jnp.int32) == forced)
    return jnp.where(heavy_dest[None, :], CAP, light).astype(jnp.int32)


def set_ends(result, own_key, low, high):
    extent = result.shape
    place = [jax.random.randint(jax.random.fold_in(own_key, axis), (), 0, extent[axis]) for axis in range(len(extent))]
    result = result.at[tuple(place)].set(low)
    longest = extent.index(max(extent))
    place[longest] = (place[longest] + 1) % extent[longest]
    return result.at[tuple(place)].set(high)


def shard_levels(key, dims, cuts, low, largest):
    def one(dim, blocks):
        draws = jax.random.uniform(jax.random.fold_in(jax.random.fold_in(key, 6), dim), (blocks,), jnp.float32, low / len(cuts), largest / len(cuts))
        return jnp.repeat(jnp.exp(draws), dims[dim] // blocks).reshape((-1,) + (1,) * (len(dims) - dim - 1))

    gain = one(*cuts[0])
    for cut in cuts[1:]:
        gain = gain * one(*cut)
    return gain


def rank_table(number_of, skew):
    weights = [(1 << 20) // math.isqrt(rank ** skew) + 1 for rank in range(1, number_of + 1)]
    width = 1 + sum(weights) // (1 << 30)
    return np.cumsum(np.array([max(1, weight // width) for weight in weights]))


def ranked_ids(rng, extent, number_of, lean):
    table = rank_table(number_of, lean)
    pick = jax.random.randint(jax.random.fold_in(rng, 1), extent, 0, int(table[number_of - 1]))
    standing = jnp.searchsorted(jnp.asarray(table, jnp.int32), pick, side="right")
    return jax.random.permutation(jax.random.fold_in(rng, 2), number_of)[standing].astype(jnp.int32)


def noise(stream_key, dims, deviation, limit, cuts=(), held_as=jnp.bfloat16):
    level = shard_levels(stream_key, dims, cuts, -0.22, 0.18) if cuts else 1.0
    array = jax.random.normal(stream_key, dims, jnp.float32) * deviation * level
    return jnp.minimum(jnp.maximum(array, -limit), limit).astype(held_as)


def setup_inputs(seed: int = 0) -> dict:
    keys = jax.random.split(jax.random.key(seed), 11)
    features = noise(keys[0], (N, D), 1.0, 6.0, ((0, 64),))
    basis_stack = noise(keys[1], (NB, D, D), D ** -0.5, 0.375, ((0, 8),))
    coeffs = noise(keys[2], (R, NB), NB ** -0.5, 0.75, ((1, 8),), jnp.float32)
    self_weight = noise(keys[3], (D, D), D ** -0.5, 0.375, ((1, 8),))
    src_row = set_ends(jax.random.randint(keys[4], (PAIRS, CAP), 0, ENT_DEV), jax.random.fold_in(keys[4], 1), 0, ENT_DEV - 1).astype(jnp.int32)
    dst_row = set_ends(jax.random.randint(keys[5], (PAIRS, CAP), 0, ENT_DEV), jax.random.fold_in(keys[5], 1), 0, ENT_DEV - 1).astype(jnp.int32)
    rel_id = set_ends(ranked_ids(keys[6], (PAIRS, CAP), R, 2), jax.random.fold_in(keys[6], 3), 0, R - 1).astype(jnp.int32)
    edge_weight = jnp.clip(jnp.exp(math.log(1.0) - 2.9957323 * jax.random.uniform(keys[7], (PAIRS, CAP), jnp.float32) ** shard_levels(keys[7], (PAIRS, CAP), ((0, 64),), -0.2, 0.2)), 0.05, 1.0)
    counts = draw_counts(jax.random.fold_in(keys[10], 71), 0)
    out_grad = noise(keys[9], (N, D), 1.0, 6.0, ((0, 64), (1, 8)))
    return dict(features=features, basis_stack=basis_stack, coeffs=coeffs, self_weight=self_weight, src_row=src_row, dst_row=dst_row, rel_id=rel_id, edge_weight=edge_weight, counts=counts, out_grad=out_grad)


def reference(features, basis_stack, coeffs, self_weight, src_row, dst_row, rel_id, edge_weight, counts, out_grad):
    shards = SHARDS
    pair_index = jnp.arange(shards * shards, dtype=jnp.int32)
    src_shard = pair_index // shards
    dst_shard = pair_index % shards
    live_slot = (jnp.arange(CAP, dtype=jnp.int32)[None, :] < counts.reshape(-1)[:, None]).astype(jnp.float32)
    slot_weight = (edge_weight * live_slot).reshape(-1)
    src_glob = (src_shard[:, None] * ENT_DEV + src_row).reshape(-1).astype(jnp.int32)
    dst_local = dst_row.reshape(shards, shards, CAP).transpose(1, 0, 2).reshape(shards * shards, CAP)
    dst_glob = (dst_shard[:, None] * ENT_DEV + dst_local).reshape(-1).astype(jnp.int32)
    relation = rel_id.reshape(-1)
    coef_edge = jnp.take(coeffs, relation, axis=0)
    slots = src_glob.shape[0]
    total_rows = features.shape[0]

    def group_step(summed, group_idx):
        def basis_step(running, basis_idx):
            position = group_idx * GROUP_BASES + basis_idx
            basis_mat = lax.dynamic_index_in_dim(basis_stack, position, 0, keepdims=False)
            zvals = jnp.dot(features, basis_mat, preferred_element_type=jnp.float32).astype(jnp.bfloat16)
            column = lax.dynamic_index_in_dim(coef_edge, position, 1, keepdims=True)
            return running + column * jnp.take(zvals, src_glob, axis=0).astype(jnp.float32), None

        running, _ = lax.scan(basis_step, jnp.zeros((slots, D), jnp.float32), jnp.arange(GROUP_BASES, dtype=jnp.int32))
        partial_value = (slot_weight[:, None] * running).astype(jnp.bfloat16)
        return summed + jax.ops.segment_sum(partial_value.astype(jnp.float32), dst_glob, num_segments=total_rows), None

    summed, _ = lax.scan(group_step, jnp.zeros((total_rows, D), jnp.float32), jnp.arange(N_REL, dtype=jnp.int32))
    preact = summed + jnp.dot(features, self_weight, preferred_element_type=jnp.float32)
    sigmoid_pre = jax.nn.sigmoid(preact)
    layer_out = (preact * sigmoid_pre).astype(jnp.bfloat16)
    grad_pre = (out_grad.astype(jnp.float32) * sigmoid_pre * (1.0 + preact * (1.0 - sigmoid_pre))).astype(jnp.bfloat16)
    grad_msg = jnp.take(grad_pre, dst_glob, axis=0).astype(jnp.float32)

    def basis_back(grad_in, position):
        basis_mat = lax.dynamic_index_in_dim(basis_stack, position, 0, keepdims=False)
        zvals = jnp.dot(features, basis_mat, preferred_element_type=jnp.float32).astype(jnp.bfloat16)
        gathered = jnp.take(zvals, src_glob, axis=0).astype(jnp.float32)
        inner_prod = jnp.sum(gathered * grad_msg, axis=1)
        coef_col = jax.ops.segment_sum(inner_prod * slot_weight, relation, num_segments=R)
        column = lax.dynamic_index_in_dim(coef_edge, position, 1, keepdims=False)
        grad_z = jax.ops.segment_sum((slot_weight * column)[:, None] * grad_msg, src_glob, num_segments=total_rows).astype(jnp.bfloat16)
        basis_g = jnp.dot(features.T, grad_z, preferred_element_type=jnp.float32)
        grad_in = grad_in + jnp.dot(grad_z, basis_mat.T, preferred_element_type=jnp.float32)
        return grad_in, (coef_col, basis_g)

    start_grad = jnp.dot(grad_pre, self_weight.T, preferred_element_type=jnp.float32)
    input_grad, (coef_cols, basis_grad) = lax.scan(basis_back, start_grad, jnp.arange(NB, dtype=jnp.int32))
    self_grad = jnp.dot(features.T, grad_pre, preferred_element_type=jnp.float32)
    return layer_out, input_grad, coef_cols.T, basis_grad, self_grad
```

```python
import jax
import jax.numpy as jnp
from jax import lax
from jax.experimental import pallas as pl
from jax.experimental.pallas import tpu as pltpu
from jax.sharding import PartitionSpec as P


F32 = jnp.float32
BF16 = jnp.bfloat16

D = 256
NE = 64
NK = 8
GB = 8
COL = 32
RELS = 1300
REL_CHUNK = 24
REL_PAD = 1344
REL_LANES = 1536
SLOTS = 2048
BLK = 256
W_ROWS = 304
G_ROWS = 80
X_ROWS = 96


def nn(a, b):
    return lax.dot_general(a, b, (((1,), (0,)), ((), ())), preferred_element_type=F32)


def nt(a, b):
    return lax.dot_general(a, b, (((1,), (1,)), ((), ())), preferred_element_type=F32)


def tn(a, b):
    return lax.dot_general(a, b, (((0,), (0,)), ((), ())), preferred_element_type=F32)


def hot(rows, index):
    place = lax.broadcasted_iota(jnp.int32, (rows, index.shape[1]), 0)
    return jnp.where(place == index, 1.0, 0.0).astype(BF16)


def call(kernel, out_shape, scratch=(), smem=0, flops=0):
    def run(*args):
        specs = [
            pl.BlockSpec(memory_space=pltpu.SMEM if n < smem else pltpu.VMEM)
            for n in range(len(args))
        ]
        return pl.pallas_call(
            kernel,
            out_shape=out_shape,
            in_specs=specs,
            out_specs=jax.tree.map(lambda _: pl.BlockSpec(memory_space=pltpu.VMEM), out_shape),
            scratch_shapes=list(scratch),
            compiler_params=pltpu.CompilerParams(vmem_limit_bytes=48 * 1024 * 1024),
            cost_estimate=pl.CostEstimate(flops=flops, bytes_accessed=4 << 20, transcendentals=0),
        )(*args)

    return run


def share_kernel(basis_ref, coef_ref, out_ref, pad_ref):
    pad_ref[...] = jnp.zeros_like(pad_ref)
    pad_ref[:, 0:RELS] = coef_ref[...]
    for l in range(GB):
        turned = basis_ref[l].astype(F32).T.astype(BF16)
        for k in range(NK):
            out_ref[k, l * COL : (l + 1) * COL, :] = turned[k * COL : (k + 1) * COL, :]
    for t in range(3):
        pair = jnp.concatenate(
            [pad_ref[:, t * 512 : t * 512 + 256], pad_ref[:, t * 512 + 256 : t * 512 + 512]], axis=0
        ).astype(BF16)
        for k in range(NK):
            out_ref[k, 256 + t * 16 : 256 + t * 16 + 16, :] = pair


def message_kernel(w_ref, x_ref, index_ref, weight_ref, out_ref, coef_ref, coef_all, z_ref, msg_ref):
    for g in range(NK):
        for t in range(3):
            pair = w_ref[g, 256 + t * 16 : 256 + t * 16 + 16, :].astype(F32)
            coef_all[g * GB : (g + 1) * GB, t * 512 : t * 512 + 256] = pair[0:8]
            coef_all[g * GB : (g + 1) * GB, t * 512 + 256 : t * 512 + 512] = pair[8:16]
        z_ref[g * 256 : (g + 1) * 256, :] = nt(w_ref[g, 0:256, :], x_ref[...]).astype(BF16)
    coef_table = coef_all[:, 0:REL_PAD].astype(BF16)

    def block(step, carry):
        lanes = pl.ds(pl.multiple_of(step * BLK, BLK), BLK)
        source = hot(256, index_ref[0:1, lanes])
        coef_ref[:, lanes] = nn(coef_table, hot(REL_PAD, index_ref[2:3, lanes]))
        total = jnp.zeros((COL, BLK), F32)
        for g in range(NK):
            taken = nn(z_ref[g * 256 : (g + 1) * 256, :], source)
            for l in range(GB):
                total += coef_ref[pl.ds(g * GB + l, 1), lanes] * taken[l * COL : (l + 1) * COL, :]
        rows = pl.ds(pl.multiple_of((step // 2) * COL, COL), COL)
        part = pl.ds(pl.multiple_of((step % 2) * BLK, BLK), BLK)
        msg_ref[rows, part] = total * weight_ref[0:1, lanes]
        return carry

    lax.fori_loop(0, SLOTS // BLK, block, 0)
    out_ref[...] = msg_ref[...].T.astype(BF16)


def node_kernel(got_ref, index_ref, x_ref, self_ref, out_grad_ref, out_ref, layer_ref, grad_ref, msg_ref):
    arrived = got_ref[...].astype(F32).T.astype(BF16)
    pre = nt(self_ref[...], x_ref[...])
    for q in range(4):
        lanes = slice(q * 512, (q + 1) * 512)
        pre += nt(arrived[q * COL : (q + 1) * COL, :], hot(256, index_ref[1:2, lanes]))
    sig = jax.nn.sigmoid(pre)
    layer_ref[...] = (pre * sig).astype(BF16)
    grad = (out_grad_ref[...].astype(F32) * sig * (1.0 + pre * (1.0 - sig))).astype(BF16)
    grad_ref[...] = grad
    for q in range(4):
        lanes = slice(q * 512, (q + 1) * 512)
        msg_ref[q * COL : (q + 1) * COL, :] = nn(grad, hot(256, index_ref[1:2, lanes]))
    out_ref[...] = msg_ref[...].T.astype(BF16)


def grad_kernel(
    got_ref,
    w_ref,
    coef_ref,
    x_ref,
    index_ref,
    weight_ref,
    self_ref,
    grad_ref,
    out_ref,
    input_ref,
    z_ref,
    m_ref,
    src_ref,
    rel_ref,
    scaled_ref,
    inner_ref,
):
    x = x_ref[...]
    for g in range(NK):
        z_ref[g * 256 : (g + 1) * 256, :] = nt(w_ref[g, 0:256, :], x).astype(BF16)
    arrived = got_ref[...].astype(F32).T
    for q in range(4):
        m_ref[:, q * 512 : (q + 1) * 512] = arrived[q * COL : (q + 1) * COL, :]

    def block(step, carry):
        lanes = pl.ds(pl.multiple_of(step * BLK, BLK), BLK)
        source = hot(256, index_ref[0:1, lanes])
        src_ref[:, lanes] = source
        rel_ref[:, lanes] = hot(REL_PAD, index_ref[2:3, lanes])
        m = m_ref[:, lanes]
        weighted = m * weight_ref[0:1, lanes]
        for g in range(NK):
            taken = nn(z_ref[g * 256 : (g + 1) * 256, :], source)
            for l in range(GB):
                b = g * GB + l
                inner_ref[b : b + 1, lanes] = jnp.sum(
                    taken[l * COL : (l + 1) * COL, :] * weighted, axis=0, keepdims=True
                )
                scaled_ref[b * COL : (b + 1) * COL, lanes] = (
                    coef_ref[pl.ds(b, 1), lanes] * weighted
                ).astype(BF16)
        return carry

    lax.fori_loop(0, SLOTS // BLK, block, 0)

    turned = x.astype(F32).T.astype(BF16)
    total = tn(grad_ref[...], self_ref[...])
    for pair in range(NK // 2):
        terms = []
        for g in (2 * pair, 2 * pair + 1):
            grad_z = nt(src_ref[...], scaled_ref[g * 256 : (g + 1) * 256, :]).astype(BF16)
            total += nn(grad_z, w_ref[g, 0:256, :])
            terms.append(nn(turned, grad_z))
        for h in range(2):
            for ib in range(32):
                rows, lanes = slice(ib * 8, ib * 8 + 8), slice(h * 128, h * 128 + 128)
                out_ref[h * 32 + ib, pair * 16 : pair * 16 + 16, :] = jnp.concatenate(
                    [terms[0][rows, lanes], terms[1][rows, lanes]], axis=0
                ).astype(BF16)
    input_ref[...] = total.T.astype(BF16)

    coef = nt(rel_ref[...], inner_ref[...].astype(BF16))
    own = nt(turned, grad_ref[...])
    for n in range(NE):
        low = jnp.zeros((16, 64), F32)
        third = jnp.zeros((8, 64), F32)
        if (n + 1) * REL_CHUNK <= REL_PAD:
            low = coef[n * REL_CHUNK : n * REL_CHUNK + 16, :]
            third = coef[n * REL_CHUNK + 16 : n * REL_CHUNK + 24, :]
        rest = jnp.zeros((8, 64), F32)
        if n < 32:
            rest = jnp.concatenate([own[n * 8 : n * 8 + 8, :], jnp.zeros((8, 32), F32)], axis=1)
        high = jnp.concatenate([third, rest], axis=0)
        out_ref[n, 64:80, :] = jnp.concatenate([low, high], axis=1).astype(BF16)


def sum_kernel(got_ref, input_ref, out_ref, own_ref):
    def add(n, total):
        return total + got_ref[n].astype(F32)

    total = lax.fori_loop(0, NE, add, jnp.zeros((G_ROWS, 128), F32), unroll=8)
    own_ref[...] = total[72:80]
    for k in range(NK):
        rows = slice(k * COL, (k + 1) * COL)
        out_ref[k, 0:32, :] = input_ref[rows, 0:128]
        out_ref[k, 32:64, :] = input_ref[rows, 128:256]
        out_ref[k, 64:80, :] = jnp.concatenate([total[k * 8 : k * 8 + 8], total[64:72]], axis=0).astype(BF16)
        out_ref[k, 80:96, :] = jnp.concatenate([total[72:80], jnp.zeros((8, 128), F32)], axis=0).astype(BF16)


def merge_kernel(me_ref, got_ref, own_ref, out_ref, input_ref):
    me = me_ref[0]
    total = got_ref[0, 0:64, :].astype(F32)
    slab = got_ref[0, 64:96, :].astype(F32)
    pieces = [slab[0:8]]
    for k in range(1, NK):
        total += got_ref[k, 0:64, :].astype(F32)
        more = got_ref[k, 64:96, :].astype(F32)
        pieces.append(more[0:8])
        slab = slab + more
    input_ref[:, 0:128] = total[0:32]
    input_ref[:, 128:256] = total[32:64]
    lane = lax.broadcasted_iota(jnp.int32, (8, 128), 1)
    rows = []
    for l in range(4):
        halves = []
        for h in range(2):
            picked = jnp.zeros((8, 128), F32)
            for k in range(4):
                moved = pieces[h * 4 + k]
                if k != l:
                    moved = pltpu.roll(moved, ((k - l) * COL) % 128, 1)
                picked = jnp.where(lane // COL == k, moved, picked)
            halves.append(picked)
        rows.append(jnp.concatenate(halves, axis=0).astype(BF16))
    first = pltpu.roll(slab[8:16], lax.rem(128 - me * GB, 128), 1)
    second = pltpu.roll(slab[16:24], lax.rem(128 + 8 - me * GB, 128), 1)
    third = pltpu.roll(slab[8:16], 64 + 16 - me * GB, 1)
    rest = pltpu.roll(own_ref[...], 96, 1)
    extra = jnp.where(lane < 8, first, jnp.where(lane < 16, second, jnp.where(lane < 32, third, rest)))
    rows.append(jnp.concatenate([extra, jnp.zeros((8, 128), F32)], axis=0).astype(BF16))
    chunk = jnp.concatenate(rows, axis=0)

    def copy(n, carry):
        out_ref[n] = chunk
        return carry

    lax.fori_loop(0, NE, copy, 0, unroll=8)


def finish_kernel(got_ref, basis_ref, coef_ref, self_ref, rel_ref, own_ref):
    for h in range(2):
        for ib in range(32):
            n = h * 32 + ib
            for l in range(4):
                part = got_ref[n, l * 16 : l * 16 + 16, :].astype(F32)
                basis_ref[h * 4 + l, ib * 8 : ib * 8 + 8, 0:128] = part[0:8]
                basis_ref[h * 4 + l, ib * 8 : ib * 8 + 8, 128:256] = part[8:16]
            extra = got_ref[n, 64:80, :].astype(F32)[0:8]
            if n < 58:
                for t in range(3):
                    piece = extra if t == 0 else pltpu.roll(extra, 128 - 8 * t, 1)
                    rel_ref[n * REL_CHUNK + t * 8 : n * REL_CHUNK + t * 8 + 8, :] = piece
            if n < 32:
                own_ref[n * 8 : n * 8 + 8, :] = pltpu.roll(extra, 96, 1)
    for t in range(11):
        across = rel_ref[t * 128 : (t + 1) * 128, :].T[0:8, :]
        width = min(128, RELS - t * 128)
        coef_ref[:, t * 128 : t * 128 + width] = across[:, 0:width]
    self_ref[...] = own_ref[...].T[0:32, :]


def body(
    features,
    basis_stack,
    coeffs,
    self_weight,
    src_row,
    dst_row,
    rel_id,
    edge_weight,
    counts,
    out_grad,
):
    shape = jax.ShapeDtypeStruct
    me = lax.axis_index("rel").astype(jnp.int32).reshape(1)

    payload = call(
        share_kernel,
        shape((NK, W_ROWS, 256), BF16),
        [pltpu.VMEM((GB, REL_LANES), F32)],
    )(basis_stack, coeffs.T)
    weights = lax.all_to_all(payload, "rel", split_axis=0, concat_axis=0, tiled=True)

    def by_lane(a):
        return a.reshape(-1, NE, 4, 8).transpose(0, 2, 1, 3).reshape(-1, SLOTS)

    index = by_lane(jnp.stack([src_row, dst_row, rel_id]))
    live = jnp.arange(32, dtype=jnp.int32)[None, :] < counts[0][:, None]
    weight = by_lane(jnp.where(live, edge_weight, 0.0)[None])
    self_t = self_weight.T

    message, coef_slot = call(
        message_kernel,
        (shape((512, 128), BF16), shape((64, SLOTS), F32)),
        [pltpu.VMEM((64, REL_LANES), F32), pltpu.VMEM((SLOTS, 256), BF16), pltpu.VMEM((128, 512), F32)],
        flops=5_000_000_000,
    )(weights, features, index, weight)
    arrived = lax.all_to_all(message.reshape(NE, 8, 128), "ent", split_axis=0, concat_axis=0, tiled=True)

    back, layer_t, grad_t = call(
        node_kernel,
        (shape((512, 128), BF16), shape((COL, 256), BF16), shape((COL, 256), BF16)),
        [pltpu.VMEM((128, 512), F32)],
        flops=100_000_000,
    )(arrived.reshape(512, 128), index, features, self_t, out_grad.T)
    returned = lax.all_to_all(back.reshape(NE, 8, 128), "ent", split_axis=0, concat_axis=0, tiled=True)

    terms, input_t = call(
        grad_kernel,
        (shape((NE, G_ROWS, 128), BF16), shape((256, 256), BF16)),
        [
            pltpu.VMEM((SLOTS, 256), BF16),
            pltpu.VMEM((COL, SLOTS), F32),
            pltpu.VMEM((256, SLOTS), BF16),
            pltpu.VMEM((REL_PAD, SLOTS), BF16),
            pltpu.VMEM((SLOTS, SLOTS), BF16),
            pltpu.VMEM((64, SLOTS), F32),
        ],
        flops=8_000_000_000,
    )(returned.reshape(512, 128), weights, coef_slot, features, index, weight, self_t, grad_t)
    terms = lax.all_to_all(terms, "ent", split_axis=0, concat_axis=0, tiled=True)

    chunk, own = call(
        sum_kernel,
        (shape((NK, X_ROWS, 128), BF16), shape((8, 128), F32)),
    )(terms, input_t)
    chunk = lax.all_to_all(chunk, "rel", split_axis=0, concat_axis=0, tiled=True)

    merged, input_grad_t = call(
        merge_kernel,
        (shape((NE, G_ROWS, 128), BF16), shape((COL, 256), F32)),
        smem=1,
    )(me, chunk, own)
    gathered = lax.all_to_all(merged, "ent", split_axis=0, concat_axis=0, tiled=True)

    basis_grad, coef_t, self_grad_t = call(
        finish_kernel,
        (shape((GB, 256, 256), F32), shape((GB, RELS), F32), shape((COL, 256), F32)),
        [pltpu.VMEM((11 * 128, 128), F32), pltpu.VMEM((256, 128), F32)],
    )(gathered)
    return (layer_t.T, input_grad_t.T, coef_t.T, basis_grad, self_grad_t.T)


def solution(mesh):
    return jax.shard_map(
        body,
        mesh=mesh,
        in_specs=(
            P("ent", None),
            P("rel", None, None),
            P(None, "rel"),
            P(None, "rel"),
            P("ent", None),
            P("ent", None),
            P("ent", None),
            P("ent", None),
            P("ent", None),
            P("ent", "rel"),
        ),
        out_specs=(
            P("ent", "rel"),
            P("ent", "rel"),
            P(None, "rel"),
            P("rel", None, None),
            P(None, "rel"),
        ),
        check_vma=False,
    )
```

```python
import jax
import jax.numpy as jnp
from jax import lax
from jax.experimental import pallas as pl
from jax.experimental.pallas import tpu as pltpu
from jax.sharding import PartitionSpec as P


F32 = jnp.float32
BF16 = jnp.bfloat16

NE = 64
NK = 8
GB = 8
COL = 32
RELS = 1300
REL_CHUNK = 24
REL_PAD = 1344
REL_LANES = 1536
SLOTS = 2048
BLK = 256
W_ROWS = 304
G_TILES = 10
X_TILES = 11
F_TILES = 9


def nn(a, b):
    return lax.dot_general(a, b, (((1,), (0,)), ((), ())), preferred_element_type=F32)


def nt(a, b):
    return lax.dot_general(a, b, (((1,), (1,)), ((), ())), preferred_element_type=F32)


def tn(a, b):
    return lax.dot_general(a, b, (((0,), (0,)), ((), ())), preferred_element_type=F32)


def hot(rows, index):
    place = lax.broadcasted_iota(jnp.int32, (rows, index.shape[1]), 0)
    return jnp.where(place == index, 1.0, 0.0).astype(BF16)


def call(kernel, out_shape, scratch=(), flops=0, vmem=16, places="", out_places=""):
    space = {"s": pltpu.SMEM, "h": pltpu.HBM, "v": pltpu.VMEM}

    def spec(letters, n):
        return pl.BlockSpec(memory_space=space[letters[n] if n < len(letters) else "v"])

    def run(*args):
        outs = out_shape if isinstance(out_shape, tuple) else (out_shape,)
        results = pl.pallas_call(
            kernel,
            out_shape=outs,
            in_specs=[spec(places, n) for n in range(len(args))],
            out_specs=tuple(spec(out_places, n) for n in range(len(outs))),
            scratch_shapes=list(scratch),
            compiler_params=pltpu.CompilerParams(vmem_limit_bytes=vmem << 20),
            cost_estimate=pl.CostEstimate(flops=flops, bytes_accessed=4 << 20, transcendentals=0),
        )(*args)
        return results if len(outs) > 1 else results[0]

    return run


def share_kernel(basis_ref, coef_ref, out_ref, basis_buf, coef_buf, pad_ref, sems):
    copies = [pltpu.make_async_copy(basis_ref.at[l], basis_buf.at[l], sems.at[l]) for l in range(GB)]
    copies.append(pltpu.make_async_copy(coef_ref, coef_buf, sems.at[GB]))
    for copy in copies:
        copy.start()
    pad_ref[...] = jnp.zeros_like(pad_ref)
    for l in range(GB):
        copies[l].wait()
        turned = basis_buf[l].astype(F32).T.astype(BF16)
        for k in range(NK):
            out_ref[k, l * COL : (l + 1) * COL, :] = turned[k * COL : (k + 1) * COL, :]
    copies[GB].wait()
    pad_ref[:, 0:RELS] = coef_buf[...]
    for t in range(3):
        pair = jnp.concatenate(
            [pad_ref[:, t * 512 : t * 512 + 256], pad_ref[:, t * 512 + 256 : t * 512 + 512]], axis=0
        ).astype(BF16)
        for k in range(NK):
            out_ref[k, 256 + t * 16 : 256 + t * 16 + 16, :] = pair


def message_kernel(w_ref, x_ref, index_ref, weight_ref, out_ref, coef_ref, z_ref, coef_all, msg_ref):
    for g in range(NK):
        for t in range(3):
            pair = w_ref[g, 256 + t * 16 : 256 + t * 16 + 16, :].astype(F32)
            coef_all[g * GB : (g + 1) * GB, t * 512 : t * 512 + 256] = pair[0:8]
            coef_all[g * GB : (g + 1) * GB, t * 512 + 256 : t * 512 + 512] = pair[8:16]
        z_ref[g * 256 : (g + 1) * 256, :] = nt(w_ref[g, 0:256, :], x_ref[...]).astype(BF16)
    coef_table = coef_all[:, 0:REL_PAD].astype(BF16)
    for step in range(SLOTS // BLK):
        lanes = slice(step * BLK, (step + 1) * BLK)
        coef_ref[:, lanes] = nn(coef_table, hot(REL_PAD, index_ref[2:3, lanes]))
        source = hot(256, index_ref[0:1, lanes])
        total = jnp.zeros((COL, BLK), F32)
        for g in range(NK):
            taken = nn(z_ref[g * 256 : (g + 1) * 256, :], source)
            for l in range(GB):
                b = g * GB + l
                total += coef_ref[b : b + 1, lanes] * taken[l * COL : (l + 1) * COL, :]
        q, part = divmod(step * BLK, 512)
        msg_ref[q * COL : (q + 1) * COL, part : part + BLK] = total * weight_ref[0:1, lanes]
    out_ref[...] = msg_ref[...].T.astype(BF16)


def take_kernel(z_ref, index_ref, taken_ref, src_ref, rel_ref):
    def block(step, carry):
        lanes = pl.ds(pl.multiple_of(step * BLK, BLK), BLK)
        source = hot(256, index_ref[0:1, lanes])
        src_ref[:, lanes] = source
        rel_ref[:, lanes] = hot(REL_PAD, index_ref[2:3, lanes])
        for g in range(NK):
            rows = slice(g * 256, (g + 1) * 256)
            taken_ref[rows, lanes] = nn(z_ref[rows, :], source).astype(BF16)
        return carry

    lax.fori_loop(0, SLOTS // BLK, block, 0)


def node_kernel(got_ref, index_ref, x_ref, self_ref, out_grad_ref, out_ref, layer_ref, grad_ref, msg_ref):
    arrived = got_ref[...].astype(F32).T.astype(BF16)
    pre = nt(self_ref[...], x_ref[...])
    for q in range(4):
        lanes = slice(q * 512, (q + 1) * 512)
        pre += nt(arrived[q * COL : (q + 1) * COL, :], hot(256, index_ref[1:2, lanes]))
    sig = jax.nn.sigmoid(pre)
    layer_ref[...] = (pre * sig).astype(BF16)
    grad = (out_grad_ref[...].astype(F32) * sig * (1.0 + pre * (1.0 - sig))).astype(BF16)
    grad_ref[...] = grad
    for q in range(4):
        lanes = slice(q * 512, (q + 1) * 512)
        msg_ref[q * COL : (q + 1) * COL, :] = nn(grad, hot(256, index_ref[1:2, lanes]))
    out_ref[...] = msg_ref[...].T.astype(BF16)


def grad_kernel(
    taken_hbm,
    coef_hbm,
    src_hbm,
    rel_hbm,
    x_hbm,
    got_ref,
    weight_ref,
    grad_ref,
    grad_z_hbm,
    out_ref,
    taken_ref,
    coef_ref,
    src_ref,
    rel_ref,
    x_ref,
    grad_z_ref,
    m_ref,
    scaled_ref,
    part_ref,
    sems,
):
    pieces = [(coef_hbm, coef_ref)]
    for g in range(NK):
        rows = pl.ds(g * 256, 256)
        pieces.append((taken_hbm.at[rows], taken_ref.at[rows]))
    pieces += [(src_hbm, src_ref), (x_hbm, x_ref), (rel_hbm, rel_ref), (grad_z_ref, grad_z_hbm)]
    copies = [pltpu.make_async_copy(a, b, sems.at[n]) for n, (a, b) in enumerate(pieces)]
    for copy in copies[:12]:
        copy.start()
    arrived = got_ref[...].astype(F32).T
    for q in range(4):
        lanes = slice(q * 512, (q + 1) * 512)
        m_ref[:, lanes] = arrived[q * COL : (q + 1) * COL, :] * weight_ref[0:1, lanes]

    copies[0].wait()
    for half in range(2):
        for b in range(half * 32, half * 32 + 32, 2):
            if b % GB == 0:
                copies[1 + b // GB].wait()
            for step in range(SLOTS // BLK):
                lanes = slice(step * BLK, (step + 1) * BLK)
                m = m_ref[:, lanes]
                sums = []
                for one in (b, b + 1):
                    rows = slice(one * COL, (one + 1) * COL)
                    inner = taken_ref[rows, lanes].astype(F32) * m
                    sums.append((inner[0:8] + inner[8:16]) + (inner[16:24] + inner[24:32]))
                    scaled_ref[rows, lanes] = (coef_ref[one : one + 1, lanes] * m).astype(BF16)
                part_ref[b * 8 : b * 8 + 16, lanes] = jnp.concatenate(sums, axis=0).astype(BF16)
        if half == 0:
            copies[9].wait()
        rows = slice(half * 1024, (half + 1) * 1024)
        grad_z_ref[:, rows] = nt(src_ref[...], scaled_ref[rows, :]).astype(BF16)

    copies[12].start()
    copies[10].wait()
    turned = x_ref[...].astype(F32).T.astype(BF16)
    terms = nn(turned, grad_z_ref[...]).astype(BF16)
    for g in range(NK):
        for h in range(2):
            lanes = slice(g * 256 + h * 128, g * 256 + h * 128 + 128)
            out_ref[h * 32 : (h + 1) * 32, g] = terms[:, lanes].reshape(32, 8, 128)

    base = lax.broadcasted_iota(jnp.int32, (128, 512), 0) & 63
    fold = jnp.where(lax.broadcasted_iota(jnp.int32, (128, 512), 1) >> 3 == base, 1.0, 0.0).astype(BF16)
    copies[11].wait()
    coef = nt(rel_ref[...], nn(fold, part_ref[...]).astype(BF16))
    none = jnp.zeros((64, 256), BF16)
    own = nt(turned, jnp.concatenate([none, grad_ref[...], none[0:32]], axis=0))
    left = lax.broadcasted_iota(jnp.int32, (8, 128), 1) < 64
    empty = jnp.zeros((8, 128), F32)
    for n in range(NE):
        first = second = third = empty
        if (n + 1) * REL_CHUNK <= REL_PAD:
            first, second, third = (coef[n * REL_CHUNK + 8 * t : n * REL_CHUNK + 8 * t + 8] for t in range(3))
        rest = own[n * 8 : n * 8 + 8] if n < 32 else empty
        out_ref[n, 8] = jnp.where(left, first, third).astype(BF16)
        out_ref[n, 9] = jnp.where(left, second, rest).astype(BF16)
    copies[12].wait()


def input_kernel(grad_z_ref, w_ref, grad_ref, self_ref, input_ref):
    total = tn(grad_ref[...], self_ref[...])
    for g in range(NK):
        total += nn(grad_z_ref[:, g * 256 : (g + 1) * 256], w_ref[g, 0:256, :])
    input_ref[...] = total.T.astype(BF16)


def sum_kernel(got_ref, input_ref, out_ref, own_ref):
    def add(n, total):
        return total + got_ref[n].astype(F32)

    total = lax.fori_loop(0, NE, add, jnp.zeros((G_TILES, 8, 128), F32), unroll=8)
    own_ref[...] = total[9]
    slab = total[8:10].astype(BF16)
    for k in range(NK):
        for h in range(2):
            part = input_ref[k * COL : (k + 1) * COL, h * 128 : h * 128 + 128]
            out_ref[k, h * 4 : h * 4 + 4] = part.reshape(4, 8, 128)
        out_ref[k, 8] = total[k].astype(BF16)
        out_ref[k, 9:11] = slab


def merge_kernel(me_ref, got_ref, own_ref, out_ref, input_ref):
    me = me_ref[0]
    total = got_ref[0, 0:8].astype(F32)
    slab = got_ref[0, 9:11].astype(F32)
    pieces = [got_ref[0, 8].astype(F32)]
    for k in range(1, NK):
        total += got_ref[k, 0:8].astype(F32)
        slab += got_ref[k, 9:11].astype(F32)
        pieces.append(got_ref[k, 8].astype(F32))
    input_ref[:, 0:128] = total[0:4].reshape(32, 128)
    input_ref[:, 128:256] = total[4:8].reshape(32, 128)
    lane = lax.broadcasted_iota(jnp.int32, (8, 128), 1)
    tiles = []
    for l in range(4):
        for h in range(2):
            picked = jnp.zeros((8, 128), F32)
            for k in range(4):
                moved = pieces[h * 4 + k]
                if k != l:
                    moved = pltpu.roll(moved, ((k - l) * COL) % 128, 1)
                picked = jnp.where(lane >> 5 == k, moved, picked)
            tiles.append(picked)
    first = pltpu.roll(slab[0], lax.rem(128 - me * GB, 128), 1)
    second = pltpu.roll(slab[1], lax.rem(128 + 8 - me * GB, 128), 1)
    third = pltpu.roll(slab[0], 64 + 16 - me * GB, 1)
    rest = pltpu.roll(own_ref[...], 96, 1)
    tiles.append(jnp.where(lane < 8, first, jnp.where(lane < 16, second, jnp.where(lane < 32, third, rest))))
    chunk = jnp.stack(tiles).astype(BF16)

    def copy(n, carry):
        out_ref[n] = chunk
        return carry

    lax.fori_loop(0, NE, copy, 0, unroll=8)


def finish_kernel(got_ref, basis_ref, coef_ref, self_ref, rel_ref, own_ref):
    for n in range(NE):
        h, ib = divmod(n, 32)
        part = got_ref[n].astype(F32)
        for l in range(4):
            for o in range(2):
                basis_ref[h * 4 + l, ib * 8 : ib * 8 + 8, o * 128 : o * 128 + 128] = part[l * 2 + o]
        if n < 58:
            for t in range(3):
                piece = part[8] if t == 0 else pltpu.roll(part[8], 128 - 8 * t, 1)
                rel_ref[n * REL_CHUNK + t * 8 : n * REL_CHUNK + t * 8 + 8, :] = piece
        if n < 32:
            own_ref[n * 8 : n * 8 + 8, :] = pltpu.roll(part[8], 96, 1)
    for t in range(11):
        across = rel_ref[t * 128 : (t + 1) * 128, :].T[0:8, :]
        width = min(128, RELS - t * 128)
        coef_ref[:, t * 128 : t * 128 + width] = across[:, 0:width]
    self_ref[...] = own_ref[...].T[0:32, :]


def body(
    features,
    basis_stack,
    coeffs,
    self_weight,
    src_row,
    dst_row,
    rel_id,
    edge_weight,
    counts,
    out_grad,
):
    shape = jax.ShapeDtypeStruct
    me = lax.axis_index("rel").astype(jnp.int32).reshape(1)

    payload = call(
        share_kernel,
        shape((NK, W_ROWS, 256), BF16),
        [
            pltpu.VMEM((GB, 256, 256), BF16),
            pltpu.VMEM((GB, RELS), F32),
            pltpu.VMEM((GB, REL_LANES), F32),
            pltpu.SemaphoreType.DMA((GB + 1,)),
        ],
        places="hh",
    )(basis_stack, coeffs.T)
    weights = lax.all_to_all(payload, "rel", split_axis=0, concat_axis=0, tiled=True)

    def by_lane(a):
        return a.reshape(-1, NE, 4, 8).transpose(0, 2, 1, 3).reshape(-1, SLOTS)

    index = by_lane(jnp.stack([src_row, dst_row, rel_id]))
    live = jnp.arange(32, dtype=jnp.int32)[None, :] < counts[0][:, None]
    weight = by_lane(jnp.where(live, edge_weight, 0.0)[None])
    self_t = self_weight.T

    message, coef_slot, z = call(
        message_kernel,
        (shape((512, 128), BF16), shape((64, SLOTS), F32), shape((SLOTS, 256), BF16)),
        [pltpu.VMEM((64, REL_LANES), F32), pltpu.VMEM((128, 512), F32)],
        flops=5_000_000_000,
    )(weights, features, index, weight)
    arrived = lax.all_to_all(message.reshape(NE, 8, 128), "ent", split_axis=0, concat_axis=0, tiled=True)

    wide = shape((256, SLOTS), BF16)
    tall = shape((SLOTS, SLOTS), BF16)
    hots = shape((REL_PAD, SLOTS), BF16)
    taken, src_hot, rel_hot = call(take_kernel, (tall, wide, hots), flops=4_000_000_000, vmem=24)(z, index)
    back, layer_t, grad_t = call(
        node_kernel,
        (shape((512, 128), BF16), shape((COL, 256), BF16), shape((COL, 256), BF16)),
        [pltpu.VMEM((128, 512), F32)],
        flops=100_000_000,
    )(arrived.reshape(512, 128), index, features, self_t, out_grad.T)
    returned = lax.all_to_all(back.reshape(NE, 8, 128), "ent", split_axis=0, concat_axis=0, tiled=True)

    grad_z, terms = call(
        grad_kernel,
        (wide, shape((NE, G_TILES, 8, 128), BF16)),
        [
            pltpu.VMEM(tall.shape, BF16),
            pltpu.VMEM((64, SLOTS), F32),
            pltpu.VMEM(wide.shape, BF16),
            pltpu.VMEM(hots.shape, BF16),
            pltpu.VMEM((256, 256), BF16),
            pltpu.VMEM(wide.shape, BF16),
            pltpu.VMEM((COL, SLOTS), F32),
            pltpu.VMEM(tall.shape, BF16),
            pltpu.VMEM((512, SLOTS), BF16),
            pltpu.SemaphoreType.DMA((13,)),
        ],
        flops=8_000_000_000,
        vmem=40,
        places="hhhhh",
        out_places="h",
    )(taken, coef_slot, src_hot, rel_hot, features, returned.reshape(512, 128), weight, grad_t)
    terms = lax.all_to_all(terms, "ent", split_axis=0, concat_axis=0, tiled=True)
    input_t = call(input_kernel, shape((256, 256), BF16), flops=2_000_000_000)(grad_z, weights, grad_t, self_t)

    chunk, own = call(
        sum_kernel,
        (shape((NK, X_TILES, 8, 128), BF16), shape((8, 128), F32)),
    )(terms, input_t)
    chunk = lax.all_to_all(chunk, "rel", split_axis=0, concat_axis=0, tiled=True)

    merged, input_grad_t = call(
        merge_kernel,
        (shape((NE, F_TILES, 8, 128), BF16), shape((COL, 256), F32)),
        places="s",
    )(me, chunk, own)
    gathered = lax.all_to_all(merged, "ent", split_axis=0, concat_axis=0, tiled=True)

    basis_grad, coef_t, self_grad_t = call(
        finish_kernel,
        (shape((GB, 256, 256), F32), shape((GB, RELS), F32), shape((COL, 256), F32)),
        [pltpu.VMEM((11 * 128, 128), F32), pltpu.VMEM((256, 128), F32)],
    )(gathered)
    return (layer_t.T, input_grad_t.T, coef_t.T, basis_grad, self_grad_t.T)


def solution(mesh):
    return jax.shard_map(
        body,
        mesh=mesh,
        in_specs=(
            P("ent", None),
            P("rel", None, None),
            P(None, "rel"),
            P(None, "rel"),
            P("ent", None),
            P("ent", None),
            P("ent", None),
            P("ent", None),
            P("ent", None),
            P("ent", "rel"),
        ),
        out_specs=(
            P("ent", "rel"),
            P("ent", "rel"),
            P(None, "rel"),
            P("rel", None, None),
            P(None, "rel"),
        ),
        check_vma=False,
    )
```

```python
import jax
import jax.numpy as jnp
from jax import lax
from jax.experimental import pallas as pl
from jax.experimental.pallas import tpu as pltpu
from jax.sharding import PartitionSpec as P


F32 = jnp.float32
BF16 = jnp.bfloat16

NE = 64
NK = 8
GB = 8
COL = 32
RELS = 1300
REL_CHUNK = 24
REL_PAD = 1344
REL_LANES = 1536
SLOTS = 2048
BLK = 256
W_ROWS = 304
G_TILES = 10
X_TILES = 11
F_TILES = 9


def nn(a, b):
    return lax.dot_general(a, b, (((1,), (0,)), ((), ())), preferred_element_type=F32)


def nt(a, b):
    return lax.dot_general(a, b, (((1,), (1,)), ((), ())), preferred_element_type=F32)


def tn(a, b):
    return lax.dot_general(a, b, (((0,), (0,)), ((), ())), preferred_element_type=F32)


def hot(rows, index):
    place = lax.broadcasted_iota(jnp.int32, (rows, index.shape[1]), 0)
    return jnp.where(place == index, 1.0, 0.0).astype(BF16)


def call(kernel, out_shape, scratch=(), flops=0, vmem=60, places="", out_places=""):
    space = {"s": pltpu.SMEM, "h": pltpu.HBM, "v": pltpu.VMEM}

    def spec(letters, n):
        return pl.BlockSpec(memory_space=space[letters[n] if n < len(letters) else "v"])

    def run(*args):
        outs = out_shape if isinstance(out_shape, tuple) else (out_shape,)
        results = pl.pallas_call(
            kernel,
            out_shape=outs,
            in_specs=[spec(places, n) for n in range(len(args))],
            out_specs=tuple(spec(out_places, n) for n in range(len(outs))),
            scratch_shapes=list(scratch),
            compiler_params=pltpu.CompilerParams(vmem_limit_bytes=vmem << 20),
            cost_estimate=pl.CostEstimate(flops=flops, bytes_accessed=4 << 20, transcendentals=0),
        )(*args)
        return results if len(outs) > 1 else results[0]

    return run


def share_kernel(basis_ref, coef_ref, out_ref, basis_buf, coef_buf, pad_ref, sems):
    copies = [pltpu.make_async_copy(basis_ref.at[l], basis_buf.at[l], sems.at[l]) for l in range(GB)]
    copies.append(pltpu.make_async_copy(coef_ref, coef_buf, sems.at[GB]))
    for copy in copies:
        copy.start()
    pad_ref[...] = jnp.zeros_like(pad_ref)
    for l in range(GB):
        copies[l].wait()
        turned = basis_buf[l].astype(F32).T.astype(BF16)
        for k in range(NK):
            out_ref[k, l * COL : (l + 1) * COL, :] = turned[k * COL : (k + 1) * COL, :]
    copies[GB].wait()
    pad_ref[:, 0:RELS] = coef_buf[...]
    for t in range(3):
        pair = jnp.concatenate(
            [pad_ref[:, t * 512 : t * 512 + 256], pad_ref[:, t * 512 + 256 : t * 512 + 512]], axis=0
        ).astype(BF16)
        for k in range(NK):
            out_ref[k, 256 + t * 16 : 256 + t * 16 + 16, :] = pair


def hot_kernel(index_ref, src_ref, rel_ref):
    def block(step, carry):
        lanes = pl.ds(pl.multiple_of(step * BLK, BLK), BLK)
        src_ref[:, lanes] = hot(256, index_ref[0:1, lanes])
        rel_ref[:, lanes] = hot(REL_PAD, index_ref[2:3, lanes])
        return carry

    lax.fori_loop(0, SLOTS // BLK, block, 0)


def message_kernel(w_ref, x_ref, index_ref, weight_ref, out_ref, coef_ref, z_ref, coef_all, msg_ref):
    for g in range(NK):
        for t in range(3):
            pair = w_ref[g, 256 + t * 16 : 256 + t * 16 + 16, :].astype(F32)
            coef_all[g * GB : (g + 1) * GB, t * 512 : t * 512 + 256] = pair[0:8]
            coef_all[g * GB : (g + 1) * GB, t * 512 + 256 : t * 512 + 512] = pair[8:16]
        z_ref[g * 256 : (g + 1) * 256, :] = nt(w_ref[g, 0:256, :], x_ref[...]).astype(BF16)
    coef_table = coef_all[:, 0:REL_PAD].astype(BF16)
    for step in range(SLOTS // BLK):
        lanes = slice(step * BLK, (step + 1) * BLK)
        coef_ref[:, lanes] = nn(coef_table, hot(REL_PAD, index_ref[2:3, lanes]))
        source = hot(256, index_ref[0:1, lanes])
        total = jnp.zeros((COL, BLK), F32)
        for g in range(NK):
            taken = nn(z_ref[g * 256 : (g + 1) * 256, :], source)
            for l in range(GB):
                b = g * GB + l
                total += coef_ref[b : b + 1, lanes] * taken[l * COL : (l + 1) * COL, :]
        q, part = divmod(step * BLK, 512)
        msg_ref[q * COL : (q + 1) * COL, part : part + BLK] = total * weight_ref[0:1, lanes]
    out_ref[...] = msg_ref[...].T.astype(BF16)


def take_kernel(w_ref, x_ref, index_ref, taken_hbm, z_ref, taken_ref, sems):
    for g in range(NK):
        z_ref[g * 256 : (g + 1) * 256, :] = nt(w_ref[g, 0:256, :], x_ref[...]).astype(BF16)
    copies = []
    for g in range(NK):
        rows = slice(g * 256, (g + 1) * 256)
        for step in range(SLOTS // BLK):
            lanes = slice(step * BLK, (step + 1) * BLK)
            source = hot(256, index_ref[0:1, lanes])
            taken_ref[rows, lanes] = nn(z_ref[rows, :], source).astype(BF16)
        place = pl.ds(g * 256, 256)
        copies.append(pltpu.make_async_copy(taken_ref.at[place], taken_hbm.at[place], sems.at[g]))
        copies[g].start()
    for copy in copies:
        copy.wait()


def node_kernel(got_ref, index_ref, x_ref, self_ref, out_grad_ref, out_ref, layer_ref, grad_ref, msg_ref):
    arrived = got_ref[...].astype(F32).T.astype(BF16)
    pre = nt(self_ref[...], x_ref[...])
    for q in range(4):
        lanes = slice(q * 512, (q + 1) * 512)
        pre += nt(arrived[q * COL : (q + 1) * COL, :], hot(256, index_ref[1:2, lanes]))
    sig = jax.nn.sigmoid(pre)
    layer_ref[...] = (pre * sig).astype(BF16)
    grad = (out_grad_ref[...].astype(F32) * sig * (1.0 + pre * (1.0 - sig))).astype(BF16)
    grad_ref[...] = grad
    for q in range(4):
        lanes = slice(q * 512, (q + 1) * 512)
        msg_ref[q * COL : (q + 1) * COL, :] = nn(grad, hot(256, index_ref[1:2, lanes]))
    out_ref[...] = msg_ref[...].T.astype(BF16)


def grad_kernel(
    taken_hbm,
    coef_hbm,
    src_hbm,
    rel_hbm,
    x_hbm,
    got_ref,
    weight_ref,
    grad_ref,
    grad_z_hbm,
    out_ref,
    taken_ref,
    coef_ref,
    src_ref,
    rel_ref,
    x_ref,
    grad_z_ref,
    m_ref,
    scaled_ref,
    part_ref,
    sems,
):
    pieces = [(coef_hbm, coef_ref)]
    for g in range(NK):
        rows = pl.ds(g * 256, 256)
        pieces.append((taken_hbm.at[rows], taken_ref.at[rows]))
    pieces += [(src_hbm, src_ref), (x_hbm, x_ref), (rel_hbm, rel_ref), (grad_z_ref, grad_z_hbm)]
    copies = [pltpu.make_async_copy(a, b, sems.at[n]) for n, (a, b) in enumerate(pieces)]
    for copy in copies[:12]:
        copy.start()
    arrived = got_ref[...].astype(F32).T
    for q in range(4):
        lanes = slice(q * 512, (q + 1) * 512)
        m_ref[:, lanes] = arrived[q * COL : (q + 1) * COL, :] * weight_ref[0:1, lanes]

    copies[0].wait()
    for half in range(2):
        for b in range(half * 32, half * 32 + 32, 2):
            if b % GB == 0:
                copies[1 + b // GB].wait()
            for step in range(SLOTS // BLK):
                lanes = slice(step * BLK, (step + 1) * BLK)
                m = m_ref[:, lanes]
                sums = []
                for one in (b, b + 1):
                    rows = slice(one * COL, (one + 1) * COL)
                    inner = taken_ref[rows, lanes].astype(F32) * m
                    sums.append((inner[0:8] + inner[8:16]) + (inner[16:24] + inner[24:32]))
                    scaled_ref[rows, lanes] = (coef_ref[one : one + 1, lanes] * m).astype(BF16)
                part_ref[b * 8 : b * 8 + 16, lanes] = jnp.concatenate(sums, axis=0).astype(BF16)
        if half == 0:
            copies[9].wait()
        rows = slice(half * 1024, (half + 1) * 1024)
        grad_z_ref[:, rows] = nt(src_ref[...], scaled_ref[rows, :]).astype(BF16)

    copies[12].start()
    copies[10].wait()
    turned = x_ref[...].astype(F32).T.astype(BF16)
    terms = nn(turned, grad_z_ref[...]).astype(BF16)
    for g in range(NK):
        for h in range(2):
            lanes = slice(g * 256 + h * 128, g * 256 + h * 128 + 128)
            out_ref[h * 32 : (h + 1) * 32, g] = terms[:, lanes].reshape(32, 8, 128)

    base = lax.broadcasted_iota(jnp.int32, (128, 512), 0) & 63
    fold = jnp.where(lax.broadcasted_iota(jnp.int32, (128, 512), 1) >> 3 == base, 1.0, 0.0).astype(BF16)
    copies[11].wait()
    coef = nt(rel_ref[...], nn(fold, part_ref[...]).astype(BF16))
    none = jnp.zeros((64, 256), BF16)
    own = nt(turned, jnp.concatenate([none, grad_ref[...], none[0:32]], axis=0))
    left = lax.broadcasted_iota(jnp.int32, (8, 128), 1) < 64
    empty = jnp.zeros((8, 128), F32)
    for n in range(NE):
        first = second = third = empty
        if (n + 1) * REL_CHUNK <= REL_PAD:
            first, second, third = (coef[n * REL_CHUNK + 8 * t : n * REL_CHUNK + 8 * t + 8] for t in range(3))
        rest = own[n * 8 : n * 8 + 8] if n < 32 else empty
        out_ref[n, 8] = jnp.where(left, first, third).astype(BF16)
        out_ref[n, 9] = jnp.where(left, second, rest).astype(BF16)
    copies[12].wait()


def input_kernel(grad_z_ref, w_ref, grad_ref, self_ref, input_ref):
    total = tn(grad_ref[...], self_ref[...])
    for g in range(NK):
        total += nn(grad_z_ref[:, g * 256 : (g + 1) * 256], w_ref[g, 0:256, :])
    input_ref[...] = total.T.astype(BF16)


def sum_kernel(got_ref, input_ref, out_ref, own_ref):
    def add(n, total):
        return total + got_ref[n].astype(F32)

    total = lax.fori_loop(0, NE, add, jnp.zeros((G_TILES, 8, 128), F32), unroll=8)
    own_ref[...] = total[9]
    slab = total[8:10].astype(BF16)
    for k in range(NK):
        for h in range(2):
            part = input_ref[k * COL : (k + 1) * COL, h * 128 : h * 128 + 128]
            out_ref[k, h * 4 : h * 4 + 4] = part.reshape(4, 8, 128)
        out_ref[k, 8] = total[k].astype(BF16)
        out_ref[k, 9:11] = slab


def merge_kernel(me_ref, got_ref, own_ref, out_ref, input_ref):
    me = me_ref[0]
    total = got_ref[0, 0:8].astype(F32)
    slab = got_ref[0, 9:11].astype(F32)
    pieces = [got_ref[0, 8].astype(F32)]
    for k in range(1, NK):
        total += got_ref[k, 0:8].astype(F32)
        slab += got_ref[k, 9:11].astype(F32)
        pieces.append(got_ref[k, 8].astype(F32))
    input_ref[:, 0:128] = total[0:4].reshape(32, 128)
    input_ref[:, 128:256] = total[4:8].reshape(32, 128)
    lane = lax.broadcasted_iota(jnp.int32, (8, 128), 1)
    tiles = []
    for l in range(4):
        for h in range(2):
            picked = jnp.zeros((8, 128), F32)
            for k in range(4):
                moved = pieces[h * 4 + k]
                if k != l:
                    moved = pltpu.roll(moved, ((k - l) * COL) % 128, 1)
                picked = jnp.where(lane >> 5 == k, moved, picked)
            tiles.append(picked)
    first = pltpu.roll(slab[0], lax.rem(128 - me * GB, 128), 1)
    second = pltpu.roll(slab[1], lax.rem(128 + 8 - me * GB, 128), 1)
    third = pltpu.roll(slab[0], 64 + 16 - me * GB, 1)
    rest = pltpu.roll(own_ref[...], 96, 1)
    tiles.append(jnp.where(lane < 8, first, jnp.where(lane < 16, second, jnp.where(lane < 32, third, rest))))
    chunk = jnp.stack(tiles).astype(BF16)

    def copy(n, carry):
        out_ref[n] = chunk
        return carry

    lax.fori_loop(0, NE, copy, 0, unroll=8)


def finish_kernel(got_ref, basis_ref, coef_ref, self_ref, rel_ref, own_ref):
    for n in range(NE):
        h, ib = divmod(n, 32)
        part = got_ref[n].astype(F32)
        for l in range(4):
            for o in range(2):
                basis_ref[h * 4 + l, ib * 8 : ib * 8 + 8, o * 128 : o * 128 + 128] = part[l * 2 + o]
        if n < 58:
            for t in range(3):
                piece = part[8] if t == 0 else pltpu.roll(part[8], 128 - 8 * t, 1)
                rel_ref[n * REL_CHUNK + t * 8 : n * REL_CHUNK + t * 8 + 8, :] = piece
        if n < 32:
            own_ref[n * 8 : n * 8 + 8, :] = pltpu.roll(part[8], 96, 1)
    for t in range(11):
        across = rel_ref[t * 128 : (t + 1) * 128, :].T[0:8, :]
        width = min(128, RELS - t * 128)
        coef_ref[:, t * 128 : t * 128 + width] = across[:, 0:width]
    self_ref[...] = own_ref[...].T[0:32, :]


def body(
    features,
    basis_stack,
    coeffs,
    self_weight,
    src_row,
    dst_row,
    rel_id,
    edge_weight,
    counts,
    out_grad,
):
    shape = jax.ShapeDtypeStruct
    me = lax.axis_index("rel").astype(jnp.int32).reshape(1)

    payload = call(
        share_kernel,
        shape((NK, W_ROWS, 256), BF16),
        [
            pltpu.VMEM((GB, 256, 256), BF16),
            pltpu.VMEM((GB, RELS), F32),
            pltpu.VMEM((GB, REL_LANES), F32),
            pltpu.SemaphoreType.DMA((GB + 1,)),
        ],
        places="hh",
    )(basis_stack, coeffs.T)
    weights = lax.all_to_all(payload, "rel", split_axis=0, concat_axis=0, tiled=True)

    def by_lane(a):
        return a.reshape(-1, NE, 4, 8).transpose(0, 2, 1, 3).reshape(-1, SLOTS)

    index = by_lane(jnp.stack([src_row, dst_row, rel_id]))
    live = jnp.arange(32, dtype=jnp.int32)[None, :] < counts[0][:, None]
    weight = by_lane(jnp.where(live, edge_weight, 0.0)[None])
    self_t = self_weight.T

    wide = shape((256, SLOTS), BF16)
    tall = shape((SLOTS, SLOTS), BF16)
    hots = shape((REL_PAD, SLOTS), BF16)
    src_hot, rel_hot = call(hot_kernel, (wide, hots), flops=4_000_000_000)(index)
    message, coef_slot = call(
        message_kernel,
        (shape((512, 128), BF16), shape((64, SLOTS), F32)),
        [pltpu.VMEM((SLOTS, 256), BF16), pltpu.VMEM((64, REL_LANES), F32), pltpu.VMEM((128, 512), F32)],
        flops=5_000_000_000,
    )(weights, features, index, weight)
    arrived = lax.all_to_all(message.reshape(NE, 8, 128), "ent", split_axis=0, concat_axis=0, tiled=True)

    taken = call(
        take_kernel,
        tall,
        [pltpu.VMEM((SLOTS, 256), BF16), pltpu.VMEM(tall.shape, BF16), pltpu.SemaphoreType.DMA((NK,))],
        flops=4_000_000_000,
        out_places="h",
    )(weights, features, index)
    back, layer_t, grad_t = call(
        node_kernel,
        (shape((512, 128), BF16), shape((COL, 256), BF16), shape((COL, 256), BF16)),
        [pltpu.VMEM((128, 512), F32)],
        flops=100_000_000,
    )(arrived.reshape(512, 128), index, features, self_t, out_grad.T)
    returned = lax.all_to_all(back.reshape(NE, 8, 128), "ent", split_axis=0, concat_axis=0, tiled=True)

    grad_z, terms = call(
        grad_kernel,
        (wide, shape((NE, G_TILES, 8, 128), BF16)),
        [
            pltpu.VMEM(tall.shape, BF16),
            pltpu.VMEM((64, SLOTS), F32),
            pltpu.VMEM(wide.shape, BF16),
            pltpu.VMEM(hots.shape, BF16),
            pltpu.VMEM((256, 256), BF16),
            pltpu.VMEM(wide.shape, BF16),
            pltpu.VMEM((COL, SLOTS), F32),
            pltpu.VMEM(tall.shape, BF16),
            pltpu.VMEM((512, SLOTS), BF16),
            pltpu.SemaphoreType.DMA((13,)),
        ],
        flops=8_000_000_000,
        places="hhhhh",
        out_places="h",
    )(taken, coef_slot, src_hot, rel_hot, features, returned.reshape(512, 128), weight, grad_t)
    terms = lax.all_to_all(terms, "ent", split_axis=0, concat_axis=0, tiled=True)
    input_t = call(input_kernel, shape((256, 256), BF16), flops=2_000_000_000)(grad_z, weights, grad_t, self_t)

    chunk, own = call(
        sum_kernel,
        (shape((NK, X_TILES, 8, 128), BF16), shape((8, 128), F32)),
    )(terms, input_t)
    chunk = lax.all_to_all(chunk, "rel", split_axis=0, concat_axis=0, tiled=True)

    merged, input_grad_t = call(
        merge_kernel,
        (shape((NE, F_TILES, 8, 128), BF16), shape((COL, 256), F32)),
        places="s",
    )(me, chunk, own)
    gathered = lax.all_to_all(merged, "ent", split_axis=0, concat_axis=0, tiled=True)

    basis_grad, coef_t, self_grad_t = call(
        finish_kernel,
        (shape((GB, 256, 256), F32), shape((GB, RELS), F32), shape((COL, 256), F32)),
        [pltpu.VMEM((11 * 128, 128), F32), pltpu.VMEM((256, 128), F32)],
    )(gathered)
    return (layer_t.T, input_grad_t.T, coef_t.T, basis_grad, self_grad_t.T)


def solution(mesh):
    return jax.shard_map(
        body,
        mesh=mesh,
        in_specs=(
            P("ent", None),
            P("rel", None, None),
            P(None, "rel"),
            P(None, "rel"),
            P("ent", None),
            P("ent", None),
            P("ent", None),
            P("ent", None),
            P("ent", None),
            P("ent", "rel"),
        ),
        out_specs=(
            P("ent", "rel"),
            P("ent", "rel"),
            P(None, "rel"),
            P("rel", None, None),
            P(None, "rel"),
        ),
        check_vma=False,
    )
```

```python
import jax
import jax.numpy as jnp
from jax import lax
from jax.experimental import pallas as pl
from jax.experimental.pallas import tpu as pltpu
from jax.sharding import PartitionSpec as P


F32 = jnp.float32
BF16 = jnp.bfloat16

NE = 64
NK = 8
GB = 8
COL = 32
RELS = 1300
REL_CHUNK = 24
REL_PAD = 1344
REL_LANES = 1536
SLOTS = 2048
BLK = 256
W_ROWS = 304
G_TILES = 10
X_TILES = 11
F_TILES = 9


def nn(a, b):
    return lax.dot_general(a, b, (((1,), (0,)), ((), ())), preferred_element_type=F32)


def nt(a, b):
    return lax.dot_general(a, b, (((1,), (1,)), ((), ())), preferred_element_type=F32)


def tn(a, b):
    return lax.dot_general(a, b, (((0,), (0,)), ((), ())), preferred_element_type=F32)


def hot(rows, index):
    place = lax.broadcasted_iota(jnp.int32, (rows, index.shape[1]), 0)
    return jnp.where(place == index, 1.0, 0.0).astype(BF16)


def call(kernel, out_shape, scratch=(), flops=0, vmem=16, places="", out_places=""):
    space = {"s": pltpu.SMEM, "h": pltpu.HBM, "v": pltpu.VMEM}

    def spec(letters, n):
        return pl.BlockSpec(memory_space=space[letters[n] if n < len(letters) else "v"])

    def run(*args):
        outs = out_shape if isinstance(out_shape, tuple) else (out_shape,)
        results = pl.pallas_call(
            kernel,
            out_shape=outs,
            in_specs=[spec(places, n) for n in range(len(args))],
            out_specs=tuple(spec(out_places, n) for n in range(len(outs))),
            scratch_shapes=list(scratch),
            compiler_params=pltpu.CompilerParams(vmem_limit_bytes=vmem << 20),
            cost_estimate=pl.CostEstimate(flops=flops, bytes_accessed=4 << 20, transcendentals=0),
        )(*args)
        return results if len(outs) > 1 else results[0]

    return run


def share_kernel(basis_ref, coef_ref, out_hbm, basis_buf, coef_buf, pad_ref, out_ref, sems, out_sems):
    loads = [pltpu.make_async_copy(coef_ref, coef_buf, sems.at[GB])]
    loads += [pltpu.make_async_copy(basis_ref.at[l], basis_buf.at[l], sems.at[l]) for l in range(GB)]
    for load in loads:
        load.start()
    stores = []
    for n in range(GB + 1):
        rows = pl.ds(256, W_ROWS - 256) if n == 0 else pl.ds((n - 1) * COL, COL)
        stores.append(pltpu.make_async_copy(out_ref.at[:, rows], out_hbm.at[:, rows], out_sems.at[n]))
    pad_ref[...] = jnp.zeros_like(pad_ref)
    loads[0].wait()
    pad_ref[:, 0:RELS] = coef_buf[...]
    for t in range(3):
        pair = jnp.concatenate(
            [pad_ref[:, t * 512 : t * 512 + 256], pad_ref[:, t * 512 + 256 : t * 512 + 512]], axis=0
        ).astype(BF16)
        for k in range(NK):
            out_ref[k, 256 + t * 16 : 256 + t * 16 + 16, :] = pair
    stores[0].start()
    for l in range(GB):
        loads[l + 1].wait()
        turned = basis_buf[l].astype(F32).T.astype(BF16)
        for k in range(NK):
            out_ref[k, l * COL : (l + 1) * COL, :] = turned[k * COL : (k + 1) * COL, :]
        stores[l + 1].start()
    for store in stores:
        store.wait()


def message_kernel(w_ref, x_ref, index_ref, weight_ref, out_ref, coef_ref, z_ref, coef_all, msg_ref):
    for g in range(NK):
        for t in range(3):
            pair = w_ref[g, 256 + t * 16 : 256 + t * 16 + 16, :].astype(F32)
            coef_all[g * GB : (g + 1) * GB, t * 512 : t * 512 + 256] = pair[0:8]
            coef_all[g * GB : (g + 1) * GB, t * 512 + 256 : t * 512 + 512] = pair[8:16]
        z_ref[g * 256 : (g + 1) * 256, :] = nt(w_ref[g, 0:256, :], x_ref[...]).astype(BF16)
    coef_table = coef_all[:, 0:REL_PAD].astype(BF16)
    for step in range(SLOTS // BLK):
        lanes = slice(step * BLK, (step + 1) * BLK)
        coef_ref[:, lanes] = nn(coef_table, hot(REL_PAD, index_ref[2:3, lanes]))
        source = hot(256, index_ref[0:1, lanes])
        total = jnp.zeros((COL, BLK), F32)
        for g in range(NK):
            taken = nn(z_ref[g * 256 : (g + 1) * 256, :], source)
            for l in range(GB):
                b = g * GB + l
                total += coef_ref[b : b + 1, lanes] * taken[l * COL : (l + 1) * COL, :]
        q, part = divmod(step * BLK, 512)
        msg_ref[q * COL : (q + 1) * COL, part : part + BLK] = total * weight_ref[0:1, lanes]
    out_ref[...] = msg_ref[...].T.astype(BF16)


def node_kernel(got_ref, index_ref, x_ref, self_ref, out_grad_ref, out_ref, layer_ref, grad_ref, msg_ref):
    arrived = got_ref[...].astype(F32).T.astype(BF16)
    pre = nt(self_ref[...], x_ref[...])
    for q in range(4):
        lanes = slice(q * 512, (q + 1) * 512)
        pre += nt(arrived[q * COL : (q + 1) * COL, :], hot(256, index_ref[1:2, lanes]))
    sig = jax.nn.sigmoid(pre)
    layer_ref[...] = (pre * sig).astype(BF16)
    grad = (out_grad_ref[...].astype(F32) * sig * (1.0 + pre * (1.0 - sig))).astype(BF16)
    grad_ref[...] = grad
    for q in range(4):
        lanes = slice(q * 512, (q + 1) * 512)
        msg_ref[q * COL : (q + 1) * COL, :] = nn(grad, hot(256, index_ref[1:2, lanes]))
    out_ref[...] = msg_ref[...].T.astype(BF16)


def grad_kernel(
    got_ref,
    w_ref,
    coef_ref,
    x_ref,
    index_ref,
    weight_ref,
    self_ref,
    grad_ref,
    out_ref,
    input_ref,
    w_all,
    z_ref,
    src_ref,
    rel_ref,
    grad_z_ref,
    m_ref,
    scaled_ref,
    part_ref,
):
    arrived = got_ref[...].astype(F32).T
    for q in range(4):
        lanes = slice(q * 512, (q + 1) * 512)
        m_ref[:, lanes] = arrived[q * COL : (q + 1) * COL, :] * weight_ref[0:1, lanes]
    for g in range(NK):
        w_all[g * 256 : (g + 1) * 256, :] = w_ref[g, 0:256, :]
    z_ref[...] = nt(w_all[...], x_ref[...]).astype(BF16)

    for step in range(SLOTS // BLK):
        lanes = slice(step * BLK, (step + 1) * BLK)
        source = hot(256, index_ref[0:1, lanes])
        src_ref[:, lanes] = source
        rel_ref[:, lanes] = hot(REL_PAD, index_ref[2:3, lanes])
        m = m_ref[:, lanes]
        for g in range(NK):
            taken = nn(z_ref[g * 256 : (g + 1) * 256, :], source)
            for l in range(0, GB, 2):
                sums = []
                for one in (l, l + 1):
                    b = g * GB + one
                    inner = taken[one * COL : (one + 1) * COL, :] * m
                    sums.append((inner[0:8] + inner[8:16]) + (inner[16:24] + inner[24:32]))
                    scaled_ref[b * COL : (b + 1) * COL, lanes] = (coef_ref[b : b + 1, lanes] * m).astype(BF16)
                rows = slice((g * GB + l) * 8, (g * GB + l) * 8 + 16)
                part_ref[rows, lanes] = jnp.concatenate(sums, axis=0).astype(BF16)

    for half in range(2):
        rows = slice(half * 1024, (half + 1) * 1024)
        grad_z_ref[:, rows] = nt(src_ref[...], scaled_ref[rows, :]).astype(BF16)

    turned = x_ref[...].astype(F32).T.astype(BF16)
    terms = nn(turned, grad_z_ref[...]).astype(BF16)
    for g in range(NK):
        for h in range(2):
            lanes = slice(g * 256 + h * 128, g * 256 + h * 128 + 128)
            out_ref[h * 32 : (h + 1) * 32, g] = terms[:, lanes].reshape(32, 8, 128)

    base = lax.broadcasted_iota(jnp.int32, (128, 512), 0) & 63
    fold = jnp.where(lax.broadcasted_iota(jnp.int32, (128, 512), 1) >> 3 == base, 1.0, 0.0).astype(BF16)
    coef = nt(rel_ref[...], nn(fold, part_ref[...]).astype(BF16))
    none = jnp.zeros((64, 256), BF16)
    own = nt(turned, jnp.concatenate([none, grad_ref[...], none[0:32]], axis=0))
    left = lax.broadcasted_iota(jnp.int32, (8, 128), 1) < 64
    empty = jnp.zeros((8, 128), F32)
    for n in range(NE):
        first = second = third = empty
        if (n + 1) * REL_CHUNK <= REL_PAD:
            first, second, third = (coef[n * REL_CHUNK + 8 * t : n * REL_CHUNK + 8 * t + 8] for t in range(3))
        rest = own[n * 8 : n * 8 + 8] if n < 32 else empty
        out_ref[n, 8] = jnp.where(left, first, third).astype(BF16)
        out_ref[n, 9] = jnp.where(left, second, rest).astype(BF16)
    total = tn(grad_ref[...], self_ref[...]) + nn(grad_z_ref[...], w_all[...])
    input_ref[...] = total.T.astype(BF16)


def sum_kernel(got_ref, input_ref, out_ref, own_ref):
    def add(n, total):
        return total + got_ref[n].astype(F32)

    total = lax.fori_loop(0, NE, add, jnp.zeros((G_TILES, 8, 128), F32), unroll=8)
    own_ref[...] = total[9]
    slab = total[8:10].astype(BF16)
    for k in range(NK):
        for h in range(2):
            part = input_ref[k * COL : (k + 1) * COL, h * 128 : h * 128 + 128]
            out_ref[k, h * 4 : h * 4 + 4] = part.reshape(4, 8, 128)
        out_ref[k, 8] = total[k].astype(BF16)
        out_ref[k, 9:11] = slab


def merge_kernel(me_ref, got_ref, own_ref, out_ref, input_ref):
    me = me_ref[0]
    total = got_ref[0, 0:8].astype(F32)
    slab = got_ref[0, 9:11].astype(F32)
    pieces = [got_ref[0, 8].astype(F32)]
    for k in range(1, NK):
        total += got_ref[k, 0:8].astype(F32)
        slab += got_ref[k, 9:11].astype(F32)
        pieces.append(got_ref[k, 8].astype(F32))
    input_ref[:, 0:128] = total[0:4].reshape(32, 128)
    input_ref[:, 128:256] = total[4:8].reshape(32, 128)
    lane = lax.broadcasted_iota(jnp.int32, (8, 128), 1)
    tiles = []
    for l in range(4):
        for h in range(2):
            picked = jnp.zeros((8, 128), F32)
            for k in range(4):
                moved = pieces[h * 4 + k]
                if k != l:
                    moved = pltpu.roll(moved, ((k - l) * COL) % 128, 1)
                picked = jnp.where(lane >> 5 == k, moved, picked)
            tiles.append(picked)
    first = pltpu.roll(slab[0], lax.rem(128 - me * GB, 128), 1)
    second = pltpu.roll(slab[1], lax.rem(128 + 8 - me * GB, 128), 1)
    third = pltpu.roll(slab[0], 64 + 16 - me * GB, 1)
    rest = pltpu.roll(own_ref[...], 96, 1)
    tiles.append(jnp.where(lane < 8, first, jnp.where(lane < 16, second, jnp.where(lane < 32, third, rest))))
    chunk = jnp.stack(tiles).astype(BF16)

    def copy(n, carry):
        out_ref[n] = chunk
        return carry

    lax.fori_loop(0, NE, copy, 0, unroll=8)


def finish_kernel(got_ref, basis_ref, coef_ref, self_ref, rel_ref, own_ref):
    for n in range(NE):
        h, ib = divmod(n, 32)
        part = got_ref[n].astype(F32)
        for l in range(4):
            for o in range(2):
                basis_ref[h * 4 + l, ib * 8 : ib * 8 + 8, o * 128 : o * 128 + 128] = part[l * 2 + o]
        if n < 58:
            for t in range(3):
                piece = part[8] if t == 0 else pltpu.roll(part[8], 128 - 8 * t, 1)
                rel_ref[n * REL_CHUNK + t * 8 : n * REL_CHUNK + t * 8 + 8, :] = piece
        if n < 32:
            own_ref[n * 8 : n * 8 + 8, :] = pltpu.roll(part[8], 96, 1)
    for t in range(11):
        across = rel_ref[t * 128 : (t + 1) * 128, :].T[0:8, :]
        width = min(128, RELS - t * 128)
        coef_ref[:, t * 128 : t * 128 + width] = across[:, 0:width]
    self_ref[...] = own_ref[...].T[0:32, :]


def body(
    features,
    basis_stack,
    coeffs,
    self_weight,
    src_row,
    dst_row,
    rel_id,
    edge_weight,
    counts,
    out_grad,
):
    shape = jax.ShapeDtypeStruct
    me = lax.axis_index("rel").astype(jnp.int32).reshape(1)

    payload = call(
        share_kernel,
        shape((NK, W_ROWS, 256), BF16),
        [
            pltpu.VMEM((GB, 256, 256), BF16),
            pltpu.VMEM((GB, RELS), F32),
            pltpu.VMEM((GB, REL_LANES), F32),
            pltpu.VMEM((NK, W_ROWS, 256), BF16),
            pltpu.SemaphoreType.DMA((GB + 1,)),
            pltpu.SemaphoreType.DMA((GB + 1,)),
        ],
        vmem=60,
        places="hh",
        out_places="h",
    )(basis_stack, coeffs.T)
    weights = lax.all_to_all(payload, "rel", split_axis=0, concat_axis=0, tiled=True)

    def by_lane(a):
        return a.reshape(-1, NE, 4, 8).transpose(0, 2, 1, 3).reshape(-1, SLOTS)

    index = by_lane(jnp.stack([src_row, dst_row, rel_id]))
    live = jnp.arange(32, dtype=jnp.int32)[None, :] < counts[0][:, None]
    weight = by_lane(jnp.where(live, edge_weight, 0.0)[None])
    self_t = self_weight.T

    message, coef_slot = call(
        message_kernel,
        (shape((512, 128), BF16), shape((64, SLOTS), F32)),
        [pltpu.VMEM((SLOTS, 256), BF16), pltpu.VMEM((64, REL_LANES), F32), pltpu.VMEM((128, 512), F32)],
        flops=5_000_000_000,
    )(weights, features, index, weight)
    arrived = lax.all_to_all(message.reshape(NE, 8, 128), "ent", split_axis=0, concat_axis=0, tiled=True)

    back, layer_t, grad_t = call(
        node_kernel,
        (shape((512, 128), BF16), shape((COL, 256), BF16), shape((COL, 256), BF16)),
        [pltpu.VMEM((128, 512), F32)],
        flops=100_000_000,
    )(arrived.reshape(512, 128), index, features, self_t, out_grad.T)
    returned = lax.all_to_all(back.reshape(NE, 8, 128), "ent", split_axis=0, concat_axis=0, tiled=True)

    terms, input_t = call(
        grad_kernel,
        (shape((NE, G_TILES, 8, 128), BF16), shape((256, 256), BF16)),
        [
            pltpu.VMEM((SLOTS, 256), BF16),
            pltpu.VMEM((SLOTS, 256), BF16),
            pltpu.VMEM((256, SLOTS), BF16),
            pltpu.VMEM((REL_PAD, SLOTS), BF16),
            pltpu.VMEM((256, SLOTS), BF16),
            pltpu.VMEM((COL, SLOTS), F32),
            pltpu.VMEM((SLOTS, SLOTS), BF16),
            pltpu.VMEM((512, SLOTS), BF16),
        ],
        flops=8_000_000_000,
        vmem=32,
    )(returned.reshape(512, 128), weights, coef_slot, features, index, weight, self_t, grad_t)
    terms = lax.all_to_all(terms, "ent", split_axis=0, concat_axis=0, tiled=True)

    chunk, own = call(
        sum_kernel,
        (shape((NK, X_TILES, 8, 128), BF16), shape((8, 128), F32)),
    )(terms, input_t)
    chunk = lax.all_to_all(chunk, "rel", split_axis=0, concat_axis=0, tiled=True)

    merged, input_grad_t = call(
        merge_kernel,
        (shape((NE, F_TILES, 8, 128), BF16), shape((COL, 256), F32)),
        places="s",
    )(me, chunk, own)
    gathered = lax.all_to_all(merged, "ent", split_axis=0, concat_axis=0, tiled=True)

    basis_grad, coef_t, self_grad_t = call(
        finish_kernel,
        (shape((GB, 256, 256), F32), shape((GB, RELS), F32), shape((COL, 256), F32)),
        [pltpu.VMEM((11 * 128, 128), F32), pltpu.VMEM((256, 128), F32)],
    )(gathered)
    return (layer_t.T, input_grad_t.T, coef_t.T, basis_grad, self_grad_t.T)


def solution(mesh):
    return jax.shard_map(
        body,
        mesh=mesh,
        in_specs=(
            P("ent", None),
            P("rel", None, None),
            P(None, "rel"),
            P(None, "rel"),
            P("ent", None),
            P("ent", None),
            P("ent", None),
            P("ent", None),
            P("ent", None),
            P("ent", "rel"),
        ),
        out_specs=(
            P("ent", "rel"),
            P("ent", "rel"),
            P(None, "rel"),
            P("rel", None, None),
            P(None, "rel"),
        ),
        check_vma=False,
    )
```

```python
import jax
import jax.numpy as jnp
from jax import lax
from jax.experimental import pallas as pl
from jax.experimental.pallas import tpu as pltpu
from jax.sharding import PartitionSpec as P


F32 = jnp.float32
BF16 = jnp.bfloat16

NE = 64
SIDE = 8
NK = 8
GB = 8
COL = 32
RELS = 1300
REL_CHUNK = 24
REL_PAD = 1344
REL_LANES = 1536
SLOTS = 2048
BLK = 256
W_ROWS = 304
G_TILES = 10
X_TILES = 11
F_TILES = 9


def nn(a, b):
    return lax.dot_general(a, b, (((1,), (0,)), ((), ())), preferred_element_type=F32)


def nt(a, b):
    return lax.dot_general(a, b, (((1,), (1,)), ((), ())), preferred_element_type=F32)


def tn(a, b):
    return lax.dot_general(a, b, (((0,), (0,)), ((), ())), preferred_element_type=F32)


def hot(rows, index):
    place = lax.broadcasted_iota(jnp.int32, (rows, index.shape[1]), 0)
    return jnp.where(place == index, 1.0, 0.0).astype(BF16)


def call(kernel, out_shape, scratch=(), flops=0, vmem=16, places="", out_places=""):
    space = {"s": pltpu.SMEM, "h": pltpu.HBM, "v": pltpu.VMEM}

    def spec(letters, n):
        return pl.BlockSpec(memory_space=space[letters[n] if n < len(letters) else "v"])

    def run(*args):
        outs = out_shape if isinstance(out_shape, tuple) else (out_shape,)
        results = pl.pallas_call(
            kernel,
            out_shape=outs,
            in_specs=[spec(places, n) for n in range(len(args))],
            out_specs=tuple(spec(out_places, n) for n in range(len(outs))),
            scratch_shapes=list(scratch),
            compiler_params=pltpu.CompilerParams(vmem_limit_bytes=vmem << 20),
            cost_estimate=pl.CostEstimate(flops=flops, bytes_accessed=4 << 20, transcendentals=0),
        )(*args)
        return results if len(outs) > 1 else results[0]

    return run


def share_kernel(basis_ref, coef_ref, out_hbm, basis_buf, coef_buf, pad_ref, out_ref, sems, out_sems):
    loads = [pltpu.make_async_copy(coef_ref, coef_buf, sems.at[GB])]
    loads += [pltpu.make_async_copy(basis_ref.at[l], basis_buf.at[l], sems.at[l]) for l in range(GB)]
    for load in loads:
        load.start()
    stores = []
    for n in range(GB + 1):
        rows = pl.ds(256, W_ROWS - 256) if n == 0 else pl.ds((n - 1) * COL, COL)
        stores.append(pltpu.make_async_copy(out_ref.at[:, rows], out_hbm.at[:, rows], out_sems.at[n]))
    pad_ref[...] = jnp.zeros_like(pad_ref)
    loads[0].wait()
    pad_ref[:, 0:RELS] = coef_buf[...]
    for t in range(3):
        pair = jnp.concatenate(
            [pad_ref[:, t * 512 : t * 512 + 256], pad_ref[:, t * 512 + 256 : t * 512 + 512]], axis=0
        ).astype(BF16)
        for k in range(NK):
            out_ref[k, 256 + t * 16 : 256 + t * 16 + 16, :] = pair
    stores[0].start()
    for l in range(GB):
        loads[l + 1].wait()
        turned = basis_buf[l].astype(F32).T.astype(BF16)
        for k in range(NK):
            out_ref[k, l * COL : (l + 1) * COL, :] = turned[k * COL : (k + 1) * COL, :]
        stores[l + 1].start()
    for store in stores:
        store.wait()


def message_kernel(w_ref, x_ref, index_ref, weight_ref, out_ref, coef_ref, z_ref, coef_all, msg_ref):
    for g in range(NK):
        for t in range(3):
            pair = w_ref[g, 256 + t * 16 : 256 + t * 16 + 16, :].astype(F32)
            coef_all[g * GB : (g + 1) * GB, t * 512 : t * 512 + 256] = pair[0:8]
            coef_all[g * GB : (g + 1) * GB, t * 512 + 256 : t * 512 + 512] = pair[8:16]
        z_ref[g * 256 : (g + 1) * 256, :] = nt(w_ref[g, 0:256, :], x_ref[...]).astype(BF16)
    coef_table = coef_all[:, 0:REL_PAD].astype(BF16)
    for step in range(SLOTS // BLK):
        lanes = slice(step * BLK, (step + 1) * BLK)
        coef_ref[:, lanes] = nn(coef_table, hot(REL_PAD, index_ref[2:3, lanes]))
        source = hot(256, index_ref[0:1, lanes])
        total = jnp.zeros((COL, BLK), F32)
        for g in range(NK):
            taken = nn(z_ref[g * 256 : (g + 1) * 256, :], source)
            for l in range(GB):
                b = g * GB + l
                total += coef_ref[b : b + 1, lanes] * taken[l * COL : (l + 1) * COL, :]
        q, part = divmod(step * BLK, 512)
        msg_ref[q * COL : (q + 1) * COL, part : part + BLK] = total * weight_ref[0:1, lanes]
    out_ref[...] = msg_ref[...].T.astype(BF16)


def node_kernel(got_ref, index_ref, x_ref, self_ref, out_grad_ref, out_ref, layer_ref, grad_ref, msg_ref):
    arrived = got_ref[...].astype(F32).T.astype(BF16)
    pre = nt(self_ref[...], x_ref[...])
    for q in range(4):
        lanes = slice(q * 512, (q + 1) * 512)
        pre += nt(arrived[q * COL : (q + 1) * COL, :], hot(256, index_ref[1:2, lanes]))
    sig = jax.nn.sigmoid(pre)
    layer_ref[...] = (pre * sig).astype(BF16)
    grad = (out_grad_ref[...].astype(F32) * sig * (1.0 + pre * (1.0 - sig))).astype(BF16)
    grad_ref[...] = grad
    for q in range(4):
        lanes = slice(q * 512, (q + 1) * 512)
        msg_ref[q * COL : (q + 1) * COL, :] = nn(grad, hot(256, index_ref[1:2, lanes]))
    out_ref[...] = msg_ref[...].T.astype(BF16)


def grad_kernel(
    got_ref,
    w_ref,
    coef_ref,
    x_ref,
    index_ref,
    weight_ref,
    self_ref,
    grad_ref,
    out_ref,
    input_ref,
    w_all,
    z_ref,
    src_ref,
    rel_ref,
    grad_z_ref,
    m_ref,
    scaled_ref,
    part_ref,
):
    arrived = got_ref[...].astype(F32).T
    for q in range(4):
        lanes = slice(q * 512, (q + 1) * 512)
        m_ref[:, lanes] = arrived[q * COL : (q + 1) * COL, :] * weight_ref[0:1, lanes]
    for g in range(NK):
        w_all[g * 256 : (g + 1) * 256, :] = w_ref[g, 0:256, :]
    z_ref[...] = nt(w_all[...], x_ref[...]).astype(BF16)

    for step in range(SLOTS // BLK):
        lanes = slice(step * BLK, (step + 1) * BLK)
        source = hot(256, index_ref[0:1, lanes])
        src_ref[:, lanes] = source
        rel_ref[:, lanes] = hot(REL_PAD, index_ref[2:3, lanes])
        m = m_ref[:, lanes]
        for g in range(NK):
            taken = nn(z_ref[g * 256 : (g + 1) * 256, :], source)
            for l in range(0, GB, 2):
                sums = []
                for one in (l, l + 1):
                    b = g * GB + one
                    inner = taken[one * COL : (one + 1) * COL, :] * m
                    sums.append((inner[0:8] + inner[8:16]) + (inner[16:24] + inner[24:32]))
                    scaled_ref[b * COL : (b + 1) * COL, lanes] = (coef_ref[b : b + 1, lanes] * m).astype(BF16)
                rows = slice((g * GB + l) * 8, (g * GB + l) * 8 + 16)
                part_ref[rows, lanes] = jnp.concatenate(sums, axis=0).astype(BF16)

    for half in range(2):
        rows = slice(half * 1024, (half + 1) * 1024)
        grad_z_ref[:, rows] = nt(src_ref[...], scaled_ref[rows, :]).astype(BF16)

    turned = x_ref[...].astype(F32).T.astype(BF16)
    terms = nn(turned, grad_z_ref[...]).astype(BF16)
    for g in range(NK):
        for h in range(2):
            lanes = slice(g * 256 + h * 128, g * 256 + h * 128 + 128)
            out_ref[h * 32 : (h + 1) * 32, g] = terms[:, lanes].reshape(32, 8, 128)

    base = lax.broadcasted_iota(jnp.int32, (128, 512), 0) & 63
    fold = jnp.where(lax.broadcasted_iota(jnp.int32, (128, 512), 1) >> 3 == base, 1.0, 0.0).astype(BF16)
    coef = nt(rel_ref[...], nn(fold, part_ref[...]).astype(BF16))
    none = jnp.zeros((64, 256), BF16)
    own = nt(turned, jnp.concatenate([none, grad_ref[...], none[0:32]], axis=0))
    left = lax.broadcasted_iota(jnp.int32, (8, 128), 1) < 64
    empty = jnp.zeros((8, 128), F32)
    for n in range(NE):
        first = second = third = empty
        if (n + 1) * REL_CHUNK <= REL_PAD:
            first, second, third = (coef[n * REL_CHUNK + 8 * t : n * REL_CHUNK + 8 * t + 8] for t in range(3))
        rest = own[n * 8 : n * 8 + 8] if n < 32 else empty
        out_ref[n, 8] = jnp.where(left, first, third).astype(BF16)
        out_ref[n, 9] = jnp.where(left, second, rest).astype(BF16)
    total = tn(grad_ref[...], self_ref[...]) + nn(grad_z_ref[...], w_all[...])
    input_ref[...] = total.T.astype(BF16)


def sum_kernel(got_ref, input_ref, out_ref, own_ref):
    def add(n, total):
        return total + got_ref[n].astype(F32)

    total = lax.fori_loop(0, NE, add, jnp.zeros((G_TILES, 8, 128), F32), unroll=8)
    own_ref[...] = total[9]
    slab = total[8:10].astype(BF16)
    for k in range(NK):
        for h in range(2):
            part = input_ref[k * COL : (k + 1) * COL, h * 128 : h * 128 + 128]
            out_ref[k, h * 4 : h * 4 + 4] = part.reshape(4, 8, 128)
        out_ref[k, 8] = total[k].astype(BF16)
        out_ref[k, 9:11] = slab


def merge_kernel(me_ref, got_ref, own_ref, out_ref, input_ref):
    me = me_ref[0]
    total = got_ref[0, 0:8].astype(F32)
    slab = got_ref[0, 9:11].astype(F32)
    pieces = [got_ref[0, 8].astype(F32)]
    for k in range(1, NK):
        total += got_ref[k, 0:8].astype(F32)
        slab += got_ref[k, 9:11].astype(F32)
        pieces.append(got_ref[k, 8].astype(F32))
    input_ref[:, 0:128] = total[0:4].reshape(32, 128)
    input_ref[:, 128:256] = total[4:8].reshape(32, 128)
    lane = lax.broadcasted_iota(jnp.int32, (8, 128), 1)
    tiles = []
    for l in range(4):
        for h in range(2):
            picked = jnp.zeros((8, 128), F32)
            for k in range(4):
                moved = pieces[h * 4 + k]
                if k != l:
                    moved = pltpu.roll(moved, ((k - l) * COL) % 128, 1)
                picked = jnp.where(lane >> 5 == k, moved, picked)
            tiles.append(picked)
    first = pltpu.roll(slab[0], lax.rem(128 - me * GB, 128), 1)
    second = pltpu.roll(slab[1], lax.rem(128 + 8 - me * GB, 128), 1)
    third = pltpu.roll(slab[0], 64 + 16 - me * GB, 1)
    rest = pltpu.roll(own_ref[...], 96, 1)
    tiles.append(jnp.where(lane < 8, first, jnp.where(lane < 16, second, jnp.where(lane < 32, third, rest))))
    chunk = jnp.stack(tiles).astype(BF16)
    for n in range(SIDE):
        out_ref[n] = chunk


def copy_kernel(got_ref, out_ref):
    for n in range(SIDE):
        for m in range(SIDE):
            out_ref[n, m] = got_ref[m]


def finish_kernel(core_ref, got_ref, basis_hbm, coef_ref, self_ref, basis_ref, rel_ref, own_ref, sems):
    core = core_ref[0]
    copies = []
    for h in range(2):
        place = pl.ds(h * 4, 4)
        copies.append(pltpu.make_async_copy(basis_ref.at[place], basis_hbm.at[place], sems.at[h]))
    for n in range(NE):
        z, y = divmod(n, SIDE)
        h, ib = divmod(n, 32)
        part = got_ref[n + core * (y * SIDE + z - n)].astype(F32)
        for l in range(4):
            for o in range(2):
                basis_ref[h * 4 + l, ib * 8 : ib * 8 + 8, o * 128 : o * 128 + 128] = part[l * 2 + o]
        if n < 58:
            for t in range(3):
                piece = part[8] if t == 0 else pltpu.roll(part[8], 128 - 8 * t, 1)
                rel_ref[n * REL_CHUNK + t * 8 : n * REL_CHUNK + t * 8 + 8, :] = piece
        if n < 32:
            own_ref[n * 8 : n * 8 + 8, :] = pltpu.roll(part[8], 96, 1)
        if ib == 31:
            copies[h].start()
    for t in range(11):
        across = rel_ref[t * 128 : (t + 1) * 128, :].T[0:8, :]
        width = min(128, RELS - t * 128)
        coef_ref[:, t * 128 : t * 128 + width] = across[:, 0:width]
    self_ref[...] = own_ref[...].T[0:32, :]
    for copy in copies:
        copy.wait()


def lines(first):
    def place(z, y, rel):
        return (z * SIDE + y) * NK + rel

    groups = []
    for rel in range(NK):
        for a in range(SIDE):
            if rel % 2 == first:
                groups.append([place(a, b, rel) for b in range(SIDE)])
            else:
                groups.append([place(b, a, rel) for b in range(SIDE)])
    return groups


def line_exchange(a, first):
    return lax.all_to_all(
        a, ("ent", "rel"), split_axis=0, concat_axis=0, axis_index_groups=lines(first), tiled=True
    )


def body(
    features,
    basis_stack,
    coeffs,
    self_weight,
    src_row,
    dst_row,
    rel_id,
    edge_weight,
    counts,
    out_grad,
):
    shape = jax.ShapeDtypeStruct
    me = lax.axis_index("rel").astype(jnp.int32).reshape(1)

    payload = call(
        share_kernel,
        shape((NK, W_ROWS, 256), BF16),
        [
            pltpu.VMEM((GB, 256, 256), BF16),
            pltpu.VMEM((GB, RELS), F32),
            pltpu.VMEM((GB, REL_LANES), F32),
            pltpu.VMEM((NK, W_ROWS, 256), BF16),
            pltpu.SemaphoreType.DMA((GB + 1,)),
            pltpu.SemaphoreType.DMA((GB + 1,)),
        ],
        vmem=60,
        places="hh",
        out_places="h",
    )(basis_stack, coeffs.T)
    weights = lax.all_to_all(payload, "rel", split_axis=0, concat_axis=0, tiled=True)

    def by_lane(a):
        return a.reshape(-1, NE, 4, 8).transpose(0, 2, 1, 3).reshape(-1, SLOTS)

    index = by_lane(jnp.stack([src_row, dst_row, rel_id]))
    live = jnp.arange(32, dtype=jnp.int32)[None, :] < counts[0][:, None]
    weight = by_lane(jnp.where(live, edge_weight, 0.0)[None])
    self_t = self_weight.T

    message, coef_slot = call(
        message_kernel,
        (shape((512, 128), BF16), shape((64, SLOTS), F32)),
        [pltpu.VMEM((SLOTS, 256), BF16), pltpu.VMEM((64, REL_LANES), F32), pltpu.VMEM((128, 512), F32)],
        flops=5_000_000_000,
    )(weights, features, index, weight)
    arrived = lax.all_to_all(message.reshape(NE, 8, 128), "ent", split_axis=0, concat_axis=0, tiled=True)

    back, layer_t, grad_t = call(
        node_kernel,
        (shape((512, 128), BF16), shape((COL, 256), BF16), shape((COL, 256), BF16)),
        [pltpu.VMEM((128, 512), F32)],
        flops=100_000_000,
    )(arrived.reshape(512, 128), index, features, self_t, out_grad.T)
    returned = lax.all_to_all(back.reshape(NE, 8, 128), "ent", split_axis=0, concat_axis=0, tiled=True)

    terms, input_t = call(
        grad_kernel,
        (shape((NE, G_TILES, 8, 128), BF16), shape((256, 256), BF16)),
        [
            pltpu.VMEM((SLOTS, 256), BF16),
            pltpu.VMEM((SLOTS, 256), BF16),
            pltpu.VMEM((256, SLOTS), BF16),
            pltpu.VMEM((REL_PAD, SLOTS), BF16),
            pltpu.VMEM((256, SLOTS), BF16),
            pltpu.VMEM((COL, SLOTS), F32),
            pltpu.VMEM((SLOTS, SLOTS), BF16),
            pltpu.VMEM((512, SLOTS), BF16),
        ],
        flops=8_000_000_000,
        vmem=32,
    )(returned.reshape(512, 128), weights, coef_slot, features, index, weight, self_t, grad_t)
    terms = lax.all_to_all(terms, "ent", split_axis=0, concat_axis=0, tiled=True)

    chunk, own = call(
        sum_kernel,
        (shape((NK, X_TILES, 8, 128), BF16), shape((8, 128), F32)),
    )(terms, input_t)
    chunk = lax.all_to_all(chunk, "rel", split_axis=0, concat_axis=0, tiled=True)

    merged, input_grad_t = call(
        merge_kernel,
        (shape((SIDE, F_TILES, 8, 128), BF16), shape((COL, 256), F32)),
        places="s",
    )(me, chunk, own)
    line = line_exchange(merged, 0)
    copied = call(copy_kernel, shape((SIDE, SIDE, F_TILES, 8, 128), BF16))(line)
    gathered = line_exchange(copied, 1).reshape(NE, F_TILES, 8, 128)

    basis_grad, coef_t, self_grad_t = call(
        finish_kernel,
        (shape((GB, 256, 256), F32), shape((GB, RELS), F32), shape((COL, 256), F32)),
        [
            pltpu.VMEM((GB, 256, 256), F32),
            pltpu.VMEM((11 * 128, 128), F32),
            pltpu.VMEM((256, 128), F32),
            pltpu.SemaphoreType.DMA((2,)),
        ],
        places="s",
        out_places="h",
    )(lax.rem(me, 2), gathered)
    return (layer_t.T, input_grad_t.T, coef_t.T, basis_grad, self_grad_t.T)


def solution(mesh):
    return jax.shard_map(
        body,
        mesh=mesh,
        in_specs=(
            P("ent", None),
            P("rel", None, None),
            P(None, "rel"),
            P(None, "rel"),
            P("ent", None),
            P("ent", None),
            P("ent", None),
            P("ent", None),
            P("ent", None),
            P("ent", "rel"),
        ),
        out_specs=(
            P("ent", "rel"),
            P("ent", "rel"),
            P(None, "rel"),
            P("rel", None, None),
            P(None, "rel"),
        ),
        check_vma=False,
    )
```

```python
import jax
import jax.numpy as jnp
from jax import lax
from jax.experimental import pallas as pl
from jax.experimental.pallas import tpu as pltpu
from jax.sharding import PartitionSpec as P


F32 = jnp.float32
BF16 = jnp.bfloat16

NE = 64
NK = 8
GB = 8
COL = 32
RELS = 1300
REL_CHUNK = 24
REL_PAD = 1344
REL_LANES = 1536
SLOTS = 2048
BLK = 256
W_ROWS = 304
G_TILES = 10
X_TILES = 3
F_TILES = 9


def nn(a, b):
    return lax.dot_general(a, b, (((1,), (0,)), ((), ())), preferred_element_type=F32)


def nt(a, b):
    return lax.dot_general(a, b, (((1,), (1,)), ((), ())), preferred_element_type=F32)


def tn(a, b):
    return lax.dot_general(a, b, (((0,), (0,)), ((), ())), preferred_element_type=F32)


def hot(rows, index):
    place = lax.broadcasted_iota(jnp.int16, (rows, index.shape[1]), 0)
    return jnp.where(place == index.astype(jnp.int16), jnp.bfloat16(1), jnp.bfloat16(0))


def call(kernel, out_shape, scratch=(), flops=0, vmem=16, places="", out_places=""):
    space = {"s": pltpu.SMEM, "h": pltpu.HBM, "v": pltpu.VMEM}

    def spec(letters, n):
        return pl.BlockSpec(memory_space=space[letters[n] if n < len(letters) else "v"])

    def run(*args):
        outs = out_shape if isinstance(out_shape, tuple) else (out_shape,)
        results = pl.pallas_call(
            kernel,
            out_shape=outs,
            in_specs=[spec(places, n) for n in range(len(args))],
            out_specs=tuple(spec(out_places, n) for n in range(len(outs))),
            scratch_shapes=list(scratch),
            compiler_params=pltpu.CompilerParams(vmem_limit_bytes=vmem << 20),
            cost_estimate=pl.CostEstimate(flops=flops, bytes_accessed=4 << 20, transcendentals=0),
        )(*args)
        return results if len(outs) > 1 else results[0]

    return run


def share_kernel(basis_ref, coef_ref, out_hbm, basis_buf, coef_buf, pad_ref, out_ref, sems, out_sems):
    loads = [pltpu.make_async_copy(coef_ref, coef_buf, sems.at[GB])]
    loads += [pltpu.make_async_copy(basis_ref.at[l], basis_buf.at[l], sems.at[l]) for l in range(GB)]
    for load in loads:
        load.start()
    stores = []
    for n in range(GB + 1):
        rows = pl.ds(256, W_ROWS - 256) if n == 0 else pl.ds((n - 1) * COL, COL)
        stores.append(pltpu.make_async_copy(out_ref.at[:, rows], out_hbm.at[:, rows], out_sems.at[n]))
    pad_ref[...] = jnp.zeros_like(pad_ref)
    loads[0].wait()
    pad_ref[:, 0:RELS] = coef_buf[...]
    for t in range(3):
        pair = jnp.concatenate(
            [pad_ref[:, t * 512 : t * 512 + 256], pad_ref[:, t * 512 + 256 : t * 512 + 512]], axis=0
        ).astype(BF16)
        for k in range(NK):
            out_ref[k, 256 + t * 16 : 256 + t * 16 + 16, :] = pair
    stores[0].start()
    for l in range(GB):
        loads[l + 1].wait()
        turned = basis_buf[l].astype(F32).T.astype(BF16)
        for k in range(NK):
            out_ref[k, l * COL : (l + 1) * COL, :] = turned[k * COL : (k + 1) * COL, :]
        stores[l + 1].start()
    for store in stores:
        store.wait()


def message_kernel(w_ref, x_ref, index_ref, weight_ref, out_ref, coef_ref, z_ref, coef_all, msg_ref):
    for g in range(NK):
        for t in range(3):
            pair = w_ref[g, 256 + t * 16 : 256 + t * 16 + 16, :].astype(F32)
            coef_all[g * GB : (g + 1) * GB, t * 512 : t * 512 + 256] = pair[0:8]
            coef_all[g * GB : (g + 1) * GB, t * 512 + 256 : t * 512 + 512] = pair[8:16]
        z_ref[g * 256 : (g + 1) * 256, :] = nt(w_ref[g, 0:256, :], x_ref[...]).astype(BF16)
    coef_table = coef_all[:, 0:REL_PAD].astype(BF16)
    for step in range(SLOTS // BLK):
        lanes = slice(step * BLK, (step + 1) * BLK)
        coef_ref[:, lanes] = nn(coef_table, hot(REL_PAD, index_ref[2:3, lanes]))
        source = hot(256, index_ref[0:1, lanes])
        total = jnp.zeros((COL, BLK), F32)
        for g in range(NK):
            taken = nn(z_ref[g * 256 : (g + 1) * 256, :], source)
            for l in range(GB):
                b = g * GB + l
                total += coef_ref[b : b + 1, lanes] * taken[l * COL : (l + 1) * COL, :]
        q, part = divmod(step * BLK, 512)
        msg_ref[q * COL : (q + 1) * COL, part : part + BLK] = total * weight_ref[0:1, lanes]
    out_ref[...] = msg_ref[...].T.astype(BF16)


def node_kernel(got_ref, index_ref, x_ref, self_ref, out_grad_ref, out_ref, layer_ref, grad_ref, msg_ref):
    arrived = got_ref[...].astype(F32).T.astype(BF16)
    pre = nt(self_ref[...], x_ref[...])
    for q in range(4):
        lanes = slice(q * 512, (q + 1) * 512)
        pre += nt(arrived[q * COL : (q + 1) * COL, :], hot(256, index_ref[1:2, lanes]))
    sig = jax.nn.sigmoid(pre)
    layer_ref[...] = (pre * sig).astype(BF16)
    grad = (out_grad_ref[...].astype(F32) * sig * (1.0 + pre * (1.0 - sig))).astype(BF16)
    grad_ref[...] = grad
    for q in range(4):
        lanes = slice(q * 512, (q + 1) * 512)
        msg_ref[q * COL : (q + 1) * COL, :] = nn(grad, hot(256, index_ref[1:2, lanes]))
    out_ref[...] = msg_ref[...].T.astype(BF16)


def grad_kernel(
    got_ref,
    w_ref,
    coef_ref,
    x_ref,
    index_ref,
    weight_ref,
    self_ref,
    grad_ref,
    out_ref,
    input_ref,
    w_all,
    z_ref,
    src_ref,
    rel_ref,
    grad_z_ref,
    m_ref,
    scaled_ref,
    part_ref,
):
    arrived = got_ref[...].astype(F32).T
    for q in range(4):
        lanes = slice(q * 512, (q + 1) * 512)
        m_ref[:, lanes] = arrived[q * COL : (q + 1) * COL, :] * weight_ref[0:1, lanes]
    for g in range(NK):
        w_all[g * 256 : (g + 1) * 256, :] = w_ref[g, 0:256, :]
    z_ref[...] = nt(w_all[...], x_ref[...]).astype(BF16)

    for step in range(SLOTS // BLK):
        lanes = slice(step * BLK, (step + 1) * BLK)
        source = hot(256, index_ref[0:1, lanes])
        src_ref[:, lanes] = source
        rel_ref[:, lanes] = hot(REL_PAD, index_ref[2:3, lanes])
        m = m_ref[:, lanes]
        for g in range(NK):
            taken = nn(z_ref[g * 256 : (g + 1) * 256, :], source)
            for l in range(0, GB, 2):
                sums = []
                for one in (l, l + 1):
                    b = g * GB + one
                    inner = taken[one * COL : (one + 1) * COL, :] * m
                    sums.append((inner[0:8] + inner[8:16]) + (inner[16:24] + inner[24:32]))
                    scaled_ref[b * COL : (b + 1) * COL, lanes] = (coef_ref[b : b + 1, lanes] * m).astype(BF16)
                rows = slice((g * GB + l) * 8, (g * GB + l) * 8 + 16)
                part_ref[rows, lanes] = jnp.concatenate(sums, axis=0).astype(BF16)

    for half in range(2):
        rows = slice(half * 1024, (half + 1) * 1024)
        grad_z_ref[:, rows] = nt(src_ref[...], scaled_ref[rows, :]).astype(BF16)

    turned = x_ref[...].astype(F32).T.astype(BF16)
    terms = nn(turned, grad_z_ref[...]).astype(BF16)
    for g in range(NK):
        for h in range(2):
            lanes = slice(g * 256 + h * 128, g * 256 + h * 128 + 128)
            out_ref[h * 32 : (h + 1) * 32, g] = terms[:, lanes].reshape(32, 8, 128)

    base = lax.broadcasted_iota(jnp.int32, (128, 512), 0) & 63
    fold = jnp.where(lax.broadcasted_iota(jnp.int32, (128, 512), 1) >> 3 == base, 1.0, 0.0).astype(BF16)
    coef = nt(rel_ref[...], nn(fold, part_ref[...]).astype(BF16))
    none = jnp.zeros((64, 256), BF16)
    own = nt(turned, jnp.concatenate([none, grad_ref[...], none[0:32]], axis=0))
    left = lax.broadcasted_iota(jnp.int32, (8, 128), 1) < 64
    empty = jnp.zeros((8, 128), F32)
    for n in range(NE):
        first = second = third = empty
        if (n + 1) * REL_CHUNK <= REL_PAD:
            first, second, third = (coef[n * REL_CHUNK + 8 * t : n * REL_CHUNK + 8 * t + 8] for t in range(3))
        rest = own[n * 8 : n * 8 + 8] if n < 32 else empty
        out_ref[n, 8] = jnp.where(left, first, third).astype(BF16)
        out_ref[n, 9] = jnp.where(left, second, rest).astype(BF16)
    total = tn(grad_ref[...], self_ref[...]) + nn(grad_z_ref[...], w_all[...])
    input_ref[...] = total.T


def sum_kernel(got_ref, out_ref, own_ref):
    def add(n, total):
        return total + got_ref[n].astype(F32)

    total = lax.fori_loop(0, NE, add, jnp.zeros((G_TILES, 8, 128), F32), unroll=8)
    own_ref[...] = total[9]
    slab = total[8:10].astype(BF16)
    for k in range(NK):
        out_ref[k, 0] = total[k].astype(BF16)
        out_ref[k, 1:3] = slab


def merge_kernel(me_ref, got_ref, own_ref, out_ref):
    me = me_ref[0]
    slab = got_ref[0, 1:3].astype(F32)
    pieces = [got_ref[0, 0].astype(F32)]
    for k in range(1, NK):
        slab += got_ref[k, 1:3].astype(F32)
        pieces.append(got_ref[k, 0].astype(F32))
    lane = lax.broadcasted_iota(jnp.int32, (8, 128), 1)
    tiles = []
    for l in range(4):
        for h in range(2):
            picked = jnp.zeros((8, 128), F32)
            for k in range(4):
                moved = pieces[h * 4 + k]
                if k != l:
                    moved = pltpu.roll(moved, ((k - l) * COL) % 128, 1)
                picked = jnp.where(lane >> 5 == k, moved, picked)
            tiles.append(picked)
    first = pltpu.roll(slab[0], lax.rem(128 - me * GB, 128), 1)
    second = pltpu.roll(slab[1], lax.rem(128 + 8 - me * GB, 128), 1)
    third = pltpu.roll(slab[0], 64 + 16 - me * GB, 1)
    rest = pltpu.roll(own_ref[...], 96, 1)
    tiles.append(jnp.where(lane < 8, first, jnp.where(lane < 16, second, jnp.where(lane < 32, third, rest))))
    chunk = jnp.stack(tiles).astype(BF16)

    def copy(n, carry):
        out_ref[n] = chunk
        return carry

    lax.fori_loop(0, NE, copy, 0, unroll=8)


def finish_kernel(got_ref, basis_ref, coef_ref, self_ref, rel_ref, own_ref):
    for n in range(NE):
        h, ib = divmod(n, 32)
        part = got_ref[n].astype(F32)
        for l in range(4):
            for o in range(2):
                basis_ref[h * 4 + l, ib * 8 : ib * 8 + 8, o * 128 : o * 128 + 128] = part[l * 2 + o]
        if n < 58:
            for t in range(3):
                piece = part[8] if t == 0 else pltpu.roll(part[8], 128 - 8 * t, 1)
                rel_ref[n * REL_CHUNK + t * 8 : n * REL_CHUNK + t * 8 + 8, :] = piece
        if n < 32:
            own_ref[n * 8 : n * 8 + 8, :] = pltpu.roll(part[8], 96, 1)
    for t in range(11):
        across = rel_ref[t * 128 : (t + 1) * 128, :].T[0:8, :]
        width = min(128, RELS - t * 128)
        coef_ref[:, t * 128 : t * 128 + width] = across[:, 0:width]
    self_ref[...] = own_ref[...].T[0:32, :]


def body(
    features,
    basis_stack,
    coeffs,
    self_weight,
    src_row,
    dst_row,
    rel_id,
    edge_weight,
    counts,
    out_grad,
):
    shape = jax.ShapeDtypeStruct
    me = lax.axis_index("rel").astype(jnp.int32).reshape(1)

    payload = call(
        share_kernel,
        shape((NK, W_ROWS, 256), BF16),
        [
            pltpu.VMEM((GB, 256, 256), BF16),
            pltpu.VMEM((GB, RELS), F32),
            pltpu.VMEM((GB, REL_LANES), F32),
            pltpu.VMEM((NK, W_ROWS, 256), BF16),
            pltpu.SemaphoreType.DMA((GB + 1,)),
            pltpu.SemaphoreType.DMA((GB + 1,)),
        ],
        vmem=60,
        places="hh",
        out_places="h",
    )(basis_stack, coeffs.T)
    weights = lax.all_to_all(payload, "rel", split_axis=0, concat_axis=0, tiled=True)

    def by_lane(a):
        return a.reshape(-1, NE, 4, 8).transpose(0, 2, 1, 3).reshape(-1, SLOTS)

    index = by_lane(jnp.stack([src_row, dst_row, rel_id]))
    live = jnp.arange(32, dtype=jnp.int32)[None, :] < counts[0][:, None]
    weight = by_lane(jnp.where(live, edge_weight, 0.0)[None])
    self_t = self_weight.T

    message, coef_slot = call(
        message_kernel,
        (shape((512, 128), BF16), shape((64, SLOTS), F32)),
        [pltpu.VMEM((SLOTS, 256), BF16), pltpu.VMEM((64, REL_LANES), F32), pltpu.VMEM((128, 512), F32)],
        flops=5_000_000_000,
    )(weights, features, index, weight)
    arrived = lax.all_to_all(message.reshape(NE, 8, 128), "ent", split_axis=0, concat_axis=0, tiled=True)

    back, layer_t, grad_t = call(
        node_kernel,
        (shape((512, 128), BF16), shape((COL, 256), BF16), shape((COL, 256), BF16)),
        [pltpu.VMEM((128, 512), F32)],
        flops=100_000_000,
    )(arrived.reshape(512, 128), index, features, self_t, out_grad.T)
    returned = lax.all_to_all(back.reshape(NE, 8, 128), "ent", split_axis=0, concat_axis=0, tiled=True)

    terms, input_t = call(
        grad_kernel,
        (shape((NE, G_TILES, 8, 128), BF16), shape((256, 256), F32)),
        [
            pltpu.VMEM((SLOTS, 256), BF16),
            pltpu.VMEM((SLOTS, 256), BF16),
            pltpu.VMEM((256, SLOTS), BF16),
            pltpu.VMEM((REL_PAD, SLOTS), BF16),
            pltpu.VMEM((256, SLOTS), BF16),
            pltpu.VMEM((COL, SLOTS), F32),
            pltpu.VMEM((SLOTS, SLOTS), BF16),
            pltpu.VMEM((512, SLOTS), BF16),
        ],
        flops=8_000_000_000,
        vmem=32,
    )(returned.reshape(512, 128), weights, coef_slot, features, index, weight, self_t, grad_t)
    input_grad_t = lax.psum_scatter(input_t, "rel", scatter_dimension=0, tiled=True)
    terms = lax.all_to_all(terms, "ent", split_axis=0, concat_axis=0, tiled=True)

    chunk, own = call(
        sum_kernel,
        (shape((NK, X_TILES, 8, 128), BF16), shape((8, 128), F32)),
    )(terms)
    chunk = lax.all_to_all(chunk, "rel", split_axis=0, concat_axis=0, tiled=True)

    merged = call(merge_kernel, shape((NE, F_TILES, 8, 128), BF16), places="s")(me, chunk, own)
    gathered = lax.all_to_all(merged, "ent", split_axis=0, concat_axis=0, tiled=True)

    basis_grad, coef_t, self_grad_t = call(
        finish_kernel,
        (shape((GB, 256, 256), F32), shape((GB, RELS), F32), shape((COL, 256), F32)),
        [pltpu.VMEM((11 * 128, 128), F32), pltpu.VMEM((256, 128), F32)],
    )(gathered)
    return (layer_t.T, input_grad_t.T, coef_t.T, basis_grad, self_grad_t.T)


def solution(mesh):
    return jax.shard_map(
        body,
        mesh=mesh,
        in_specs=(
            P("ent", None),
            P("rel", None, None),
            P(None, "rel"),
            P(None, "rel"),
            P("ent", None),
            P("ent", None),
            P("ent", None),
            P("ent", None),
            P("ent", None),
            P("ent", "rel"),
        ),
        out_specs=(
            P("ent", "rel"),
            P("ent", "rel"),
            P(None, "rel"),
            P("rel", None, None),
            P(None, "rel"),
        ),
        check_vma=False,
    )
```

```python
import jax
import jax.numpy as jnp
from jax import lax
from jax.experimental import pallas as pl
from jax.experimental.pallas import tpu as pltpu
from jax.sharding import PartitionSpec as P


F32 = jnp.float32
BF16 = jnp.bfloat16

NE = 64
SIDE = 8
NK = 8
GB = 8
COL = 32
RELS = 1300
REL_CHUNK = 24
REL_PAD = 1344
REL_LANES = 1536
SLOTS = 2048
BLK = 256
W_ROWS = 304
G_TILES = 10
X_TILES = 11
F_TILES = 9


def nn(a, b):
    return lax.dot_general(a, b, (((1,), (0,)), ((), ())), preferred_element_type=F32)


def nt(a, b):
    return lax.dot_general(a, b, (((1,), (1,)), ((), ())), preferred_element_type=F32)


def tn(a, b):
    return lax.dot_general(a, b, (((0,), (0,)), ((), ())), preferred_element_type=F32)


def hot(rows, index):
    place = lax.broadcasted_iota(jnp.int16, (rows, index.shape[1]), 0)
    return jnp.where(place == index.astype(jnp.int16), jnp.bfloat16(1), jnp.bfloat16(0))


def call(kernel, out_shape, scratch=(), flops=0, vmem=16, places="", out_places=""):
    space = {"s": pltpu.SMEM, "h": pltpu.HBM, "v": pltpu.VMEM}

    def spec(letters, n):
        return pl.BlockSpec(memory_space=space[letters[n] if n < len(letters) else "v"])

    def run(*args):
        outs = out_shape if isinstance(out_shape, tuple) else (out_shape,)
        results = pl.pallas_call(
            kernel,
            out_shape=outs,
            in_specs=[spec(places, n) for n in range(len(args))],
            out_specs=tuple(spec(out_places, n) for n in range(len(outs))),
            scratch_shapes=list(scratch),
            compiler_params=pltpu.CompilerParams(vmem_limit_bytes=vmem << 20),
            cost_estimate=pl.CostEstimate(flops=flops, bytes_accessed=4 << 20, transcendentals=0),
        )(*args)
        return results if len(outs) > 1 else results[0]

    return run


def share_kernel(basis_ref, coef_ref, out_hbm, basis_buf, coef_buf, pad_ref, out_ref, sems, out_sems):
    loads = [pltpu.make_async_copy(coef_ref, coef_buf, sems.at[GB])]
    loads += [pltpu.make_async_copy(basis_ref.at[l], basis_buf.at[l], sems.at[l]) for l in range(GB)]
    for load in loads:
        load.start()
    stores = []
    for n in range(GB + 1):
        rows = pl.ds(256, W_ROWS - 256) if n == 0 else pl.ds((n - 1) * COL, COL)
        stores.append(pltpu.make_async_copy(out_ref.at[:, rows], out_hbm.at[:, rows], out_sems.at[n]))
    pad_ref[...] = jnp.zeros_like(pad_ref)
    loads[0].wait()
    pad_ref[:, 0:RELS] = coef_buf[...]
    for t in range(3):
        pair = jnp.concatenate(
            [pad_ref[:, t * 512 : t * 512 + 256], pad_ref[:, t * 512 + 256 : t * 512 + 512]], axis=0
        ).astype(BF16)
        for k in range(NK):
            out_ref[k, 256 + t * 16 : 256 + t * 16 + 16, :] = pair
    stores[0].start()
    for l in range(GB):
        loads[l + 1].wait()
        turned = basis_buf[l].astype(F32).T.astype(BF16)
        for k in range(NK):
            out_ref[k, l * COL : (l + 1) * COL, :] = turned[k * COL : (k + 1) * COL, :]
        stores[l + 1].start()
    for store in stores:
        store.wait()


def message_kernel(w_ref, x_ref, index_ref, weight_ref, out_ref, coef_ref, z_ref, coef_all, msg_ref):
    for g in range(NK):
        for t in range(3):
            pair = w_ref[g, 256 + t * 16 : 256 + t * 16 + 16, :].astype(F32)
            coef_all[g * GB : (g + 1) * GB, t * 512 : t * 512 + 256] = pair[0:8]
            coef_all[g * GB : (g + 1) * GB, t * 512 + 256 : t * 512 + 512] = pair[8:16]
        z_ref[g * 256 : (g + 1) * 256, :] = nt(w_ref[g, 0:256, :], x_ref[...]).astype(BF16)
    coef_table = coef_all[:, 0:REL_PAD].astype(BF16)
    for step in range(SLOTS // BLK):
        lanes = slice(step * BLK, (step + 1) * BLK)
        coef_ref[:, lanes] = nn(coef_table, hot(REL_PAD, index_ref[2:3, lanes]))
        source = hot(256, index_ref[0:1, lanes])
        total = jnp.zeros((COL, BLK), F32)
        for g in range(NK):
            taken = nn(z_ref[g * 256 : (g + 1) * 256, :], source)
            for l in range(GB):
                b = g * GB + l
                total += coef_ref[b : b + 1, lanes] * taken[l * COL : (l + 1) * COL, :]
        q, part = divmod(step * BLK, 512)
        msg_ref[q * COL : (q + 1) * COL, part : part + BLK] = total * weight_ref[0:1, lanes]
    out_ref[...] = msg_ref[...].T.astype(BF16)


def node_kernel(got_ref, index_ref, x_ref, self_ref, out_grad_ref, out_ref, layer_ref, grad_ref, msg_ref):
    arrived = got_ref[...].astype(F32).T.astype(BF16)
    pre = nt(self_ref[...], x_ref[...])
    for q in range(4):
        lanes = slice(q * 512, (q + 1) * 512)
        pre += nt(arrived[q * COL : (q + 1) * COL, :], hot(256, index_ref[1:2, lanes]))
    sig = jax.nn.sigmoid(pre)
    layer_ref[...] = (pre * sig).astype(BF16)
    grad = (out_grad_ref[...].astype(F32) * sig * (1.0 + pre * (1.0 - sig))).astype(BF16)
    grad_ref[...] = grad
    for q in range(4):
        lanes = slice(q * 512, (q + 1) * 512)
        msg_ref[q * COL : (q + 1) * COL, :] = nn(grad, hot(256, index_ref[1:2, lanes]))
    out_ref[...] = msg_ref[...].T.astype(BF16)


def grad_kernel(
    got_ref,
    w_ref,
    coef_ref,
    x_ref,
    index_ref,
    weight_ref,
    self_ref,
    grad_ref,
    out_ref,
    input_ref,
    w_all,
    z_ref,
    src_ref,
    rel_ref,
    grad_z_ref,
    m_ref,
    scaled_ref,
    part_ref,
):
    arrived = got_ref[...].astype(F32).T
    for q in range(4):
        lanes = slice(q * 512, (q + 1) * 512)
        m_ref[:, lanes] = arrived[q * COL : (q + 1) * COL, :] * weight_ref[0:1, lanes]
    for g in range(NK):
        w_all[g * 256 : (g + 1) * 256, :] = w_ref[g, 0:256, :]
    z_ref[...] = nt(w_all[...], x_ref[...]).astype(BF16)

    for step in range(SLOTS // BLK):
        lanes = slice(step * BLK, (step + 1) * BLK)
        source = hot(256, index_ref[0:1, lanes])
        src_ref[:, lanes] = source
        rel_ref[:, lanes] = hot(REL_PAD, index_ref[2:3, lanes])
        m = m_ref[:, lanes]
        for g in range(NK):
            taken = nn(z_ref[g * 256 : (g + 1) * 256, :], source)
            for l in range(0, GB, 2):
                sums = []
                for one in (l, l + 1):
                    b = g * GB + one
                    inner = taken[one * COL : (one + 1) * COL, :] * m
                    sums.append((inner[0:8] + inner[8:16]) + (inner[16:24] + inner[24:32]))
                    scaled_ref[b * COL : (b + 1) * COL, lanes] = (coef_ref[b : b + 1, lanes] * m).astype(BF16)
                rows = slice((g * GB + l) * 8, (g * GB + l) * 8 + 16)
                part_ref[rows, lanes] = jnp.concatenate(sums, axis=0).astype(BF16)

    for half in range(2):
        rows = slice(half * 1024, (half + 1) * 1024)
        grad_z_ref[:, rows] = nt(src_ref[...], scaled_ref[rows, :]).astype(BF16)

    turned = x_ref[...].astype(F32).T.astype(BF16)
    terms = nn(turned, grad_z_ref[...]).astype(BF16)
    for g in range(NK):
        for h in range(2):
            lanes = slice(g * 256 + h * 128, g * 256 + h * 128 + 128)
            out_ref[h * 32 : (h + 1) * 32, g] = terms[:, lanes].reshape(32, 8, 128)

    base = lax.broadcasted_iota(jnp.int32, (128, 512), 0) & 63
    fold = jnp.where(lax.broadcasted_iota(jnp.int32, (128, 512), 1) >> 3 == base, 1.0, 0.0).astype(BF16)
    coef = nt(rel_ref[...], nn(fold, part_ref[...]).astype(BF16))
    none = jnp.zeros((64, 256), BF16)
    own = nt(turned, jnp.concatenate([none, grad_ref[...], none[0:32]], axis=0))
    left = lax.broadcasted_iota(jnp.int32, (8, 128), 1) < 64
    empty = jnp.zeros((8, 128), F32)
    for n in range(NE):
        first = second = third = empty
        if (n + 1) * REL_CHUNK <= REL_PAD:
            first, second, third = (coef[n * REL_CHUNK + 8 * t : n * REL_CHUNK + 8 * t + 8] for t in range(3))
        rest = own[n * 8 : n * 8 + 8] if n < 32 else empty
        out_ref[n, 8] = jnp.where(left, first, third).astype(BF16)
        out_ref[n, 9] = jnp.where(left, second, rest).astype(BF16)
    total = tn(grad_ref[...], self_ref[...]) + nn(grad_z_ref[...], w_all[...])
    input_ref[...] = total.T.astype(BF16)


def sum_kernel(got_ref, input_ref, out_ref, own_ref):
    def add(n, total):
        return total + got_ref[n].astype(F32)

    total = lax.fori_loop(0, NE, add, jnp.zeros((G_TILES, 8, 128), F32), unroll=8)
    own_ref[...] = total[9]
    slab = total[8:10].astype(BF16)
    for k in range(NK):
        for h in range(2):
            part = input_ref[k * COL : (k + 1) * COL, h * 128 : h * 128 + 128]
            out_ref[k, h * 4 : h * 4 + 4] = part.reshape(4, 8, 128)
        out_ref[k, 8] = total[k].astype(BF16)
        out_ref[k, 9:11] = slab


def merge_kernel(me_ref, got_ref, own_ref, out_ref, input_ref):
    me = me_ref[0]
    total = got_ref[0, 0:8].astype(F32)
    slab = got_ref[0, 9:11].astype(F32)
    pieces = [got_ref[0, 8].astype(F32)]
    for k in range(1, NK):
        total += got_ref[k, 0:8].astype(F32)
        slab += got_ref[k, 9:11].astype(F32)
        pieces.append(got_ref[k, 8].astype(F32))
    input_ref[:, 0:128] = total[0:4].reshape(32, 128)
    input_ref[:, 128:256] = total[4:8].reshape(32, 128)
    lane = lax.broadcasted_iota(jnp.int32, (8, 128), 1)
    tiles = []
    for l in range(4):
        for h in range(2):
            picked = jnp.zeros((8, 128), F32)
            for k in range(4):
                moved = pieces[h * 4 + k]
                if k != l:
                    moved = pltpu.roll(moved, ((k - l) * COL) % 128, 1)
                picked = jnp.where(lane >> 5 == k, moved, picked)
            tiles.append(picked)
    first = pltpu.roll(slab[0], lax.rem(128 - me * GB, 128), 1)
    second = pltpu.roll(slab[1], lax.rem(128 + 8 - me * GB, 128), 1)
    third = pltpu.roll(slab[0], 64 + 16 - me * GB, 1)
    rest = pltpu.roll(own_ref[...], 96, 1)
    tiles.append(jnp.where(lane < 8, first, jnp.where(lane < 16, second, jnp.where(lane < 32, third, rest))))
    chunk = jnp.stack(tiles).astype(BF16)
    for n in range(SIDE):
        out_ref[n] = chunk


def copy_kernel(got_ref, out_hbm, sems):
    copies = [pltpu.make_async_copy(got_ref, out_hbm.at[n], sems.at[n]) for n in range(SIDE)]
    for copy in copies:
        copy.start()
    for copy in copies:
        copy.wait()


def finish_kernel(core_ref, got_ref, basis_ref, coef_ref, self_ref, rel_ref, own_ref):
    def spread(place):
        for n in range(NE):
            h, ib = divmod(n, 32)
            part = got_ref[place(*divmod(n, SIDE))].astype(F32)
            for l in range(4):
                for o in range(2):
                    basis_ref[h * 4 + l, ib * 8 : ib * 8 + 8, o * 128 : o * 128 + 128] = part[l * 2 + o]
            if n < 58:
                for t in range(3):
                    piece = part[8] if t == 0 else pltpu.roll(part[8], 128 - 8 * t, 1)
                    rel_ref[n * REL_CHUNK + t * 8 : n * REL_CHUNK + t * 8 + 8, :] = piece
            if n < 32:
                own_ref[n * 8 : n * 8 + 8, :] = pltpu.roll(part[8], 96, 1)

    @pl.when(core_ref[0] == 0)
    def _():
        spread(lambda z, y: z * SIDE + y)

    @pl.when(core_ref[0] == 1)
    def _():
        spread(lambda z, y: y * SIDE + z)

    for t in range(11):
        across = rel_ref[t * 128 : (t + 1) * 128, :].T[0:8, :]
        width = min(128, RELS - t * 128)
        coef_ref[:, t * 128 : t * 128 + width] = across[:, 0:width]
    self_ref[...] = own_ref[...].T[0:32, :]


def lines(first):
    def place(z, y, rel):
        return (z * SIDE + y) * NK + rel

    groups = []
    for rel in range(NK):
        for a in range(SIDE):
            if rel % 2 == first:
                groups.append([place(a, b, rel) for b in range(SIDE)])
            else:
                groups.append([place(b, a, rel) for b in range(SIDE)])
    return groups


def line_exchange(a, first):
    return lax.all_to_all(
        a, ("ent", "rel"), split_axis=0, concat_axis=0, axis_index_groups=lines(first), tiled=True
    )


def body(
    features,
    basis_stack,
    coeffs,
    self_weight,
    src_row,
    dst_row,
    rel_id,
    edge_weight,
    counts,
    out_grad,
):
    shape = jax.ShapeDtypeStruct
    me = lax.axis_index("rel").astype(jnp.int32).reshape(1)

    payload = call(
        share_kernel,
        shape((NK, W_ROWS, 256), BF16),
        [
            pltpu.VMEM((GB, 256, 256), BF16),
            pltpu.VMEM((GB, RELS), F32),
            pltpu.VMEM((GB, REL_LANES), F32),
            pltpu.VMEM((NK, W_ROWS, 256), BF16),
            pltpu.SemaphoreType.DMA((GB + 1,)),
            pltpu.SemaphoreType.DMA((GB + 1,)),
        ],
        vmem=60,
        places="hh",
        out_places="h",
    )(basis_stack, coeffs.T)
    weights = lax.all_to_all(payload, "rel", split_axis=0, concat_axis=0, tiled=True)

    def by_lane(a):
        return a.reshape(-1, NE, 4, 8).transpose(0, 2, 1, 3).reshape(-1, SLOTS)

    index = by_lane(jnp.stack([src_row, dst_row, rel_id]))
    live = jnp.arange(32, dtype=jnp.int32)[None, :] < counts[0][:, None]
    weight = by_lane(jnp.where(live, edge_weight, 0.0)[None])
    self_t = self_weight.T

    message, coef_slot = call(
        message_kernel,
        (shape((512, 128), BF16), shape((64, SLOTS), F32)),
        [pltpu.VMEM((SLOTS, 256), BF16), pltpu.VMEM((64, REL_LANES), F32), pltpu.VMEM((128, 512), F32)],
        flops=5_000_000_000,
    )(weights, features, index, weight)
    arrived = lax.all_to_all(message.reshape(NE, 8, 128), "ent", split_axis=0, concat_axis=0, tiled=True)

    back, layer_t, grad_t = call(
        node_kernel,
        (shape((512, 128), BF16), shape((COL, 256), BF16), shape((COL, 256), BF16)),
        [pltpu.VMEM((128, 512), F32)],
        flops=100_000_000,
    )(arrived.reshape(512, 128), index, features, self_t, out_grad.T)
    returned = lax.all_to_all(back.reshape(NE, 8, 128), "ent", split_axis=0, concat_axis=0, tiled=True)

    terms, input_t = call(
        grad_kernel,
        (shape((NE, G_TILES, 8, 128), BF16), shape((256, 256), BF16)),
        [
            pltpu.VMEM((SLOTS, 256), BF16),
            pltpu.VMEM((SLOTS, 256), BF16),
            pltpu.VMEM((256, SLOTS), BF16),
            pltpu.VMEM((REL_PAD, SLOTS), BF16),
            pltpu.VMEM((256, SLOTS), BF16),
            pltpu.VMEM((COL, SLOTS), F32),
            pltpu.VMEM((SLOTS, SLOTS), BF16),
            pltpu.VMEM((512, SLOTS), BF16),
        ],
        flops=8_000_000_000,
        vmem=32,
    )(returned.reshape(512, 128), weights, coef_slot, features, index, weight, self_t, grad_t)
    terms = lax.all_to_all(terms, "ent", split_axis=0, concat_axis=0, tiled=True)

    chunk, own = call(
        sum_kernel,
        (shape((NK, X_TILES, 8, 128), BF16), shape((8, 128), F32)),
    )(terms, input_t)
    chunk = lax.all_to_all(chunk, "rel", split_axis=0, concat_axis=0, tiled=True)

    merged, input_grad_t = call(
        merge_kernel,
        (shape((SIDE, F_TILES, 8, 128), BF16), shape((COL, 256), F32)),
        places="s",
    )(me, chunk, own)
    line = line_exchange(merged, 0)
    copied = call(
        copy_kernel,
        shape((SIDE, SIDE, F_TILES, 8, 128), BF16),
        [pltpu.SemaphoreType.DMA((SIDE,))],
        out_places="h",
    )(line)
    gathered = line_exchange(copied, 1).reshape(NE, F_TILES, 8, 128)

    basis_grad, coef_t, self_grad_t = call(
        finish_kernel,
        (shape((GB, 256, 256), F32), shape((GB, RELS), F32), shape((COL, 256), F32)),
        [pltpu.VMEM((11 * 128, 128), F32), pltpu.VMEM((256, 128), F32)],
        places="s",
    )(lax.rem(me, 2), gathered)
    return (layer_t.T, input_grad_t.T, coef_t.T, basis_grad, self_grad_t.T)


def solution(mesh):
    return jax.shard_map(
        body,
        mesh=mesh,
        in_specs=(
            P("ent", None),
            P("rel", None, None),
            P(None, "rel"),
            P(None, "rel"),
            P("ent", None),
            P("ent", None),
            P("ent", None),
            P("ent", None),
            P("ent", None),
            P("ent", "rel"),
        ),
        out_specs=(
            P("ent", "rel"),
            P("ent", "rel"),
            P(None, "rel"),
            P("rel", None, None),
            P(None, "rel"),
        ),
        check_vma=False,
    )
```
